128 devices in a mesh: segment: 4 (over x), tensor: 16 (over z, y), dp: 2 (over core).
Axes of the slice: x: 4, y: 4, z: 4, core: 2. Of those that a mesh axis runs over, the one named last changes fastest.
Arguments:
- act_input: bfloat16 [4, 384, 12288], P('dp', None, 'tensor'), may hold values from -6 to 6
- cotangent: bfloat16 [4, 384, 12288], P('dp', None, 'tensor'), may hold values from -7.2 to 7.2
- lengths: int32 [4], P('dp'), may hold values from 1 to 384, 960 in all
- clip_scale: float32 [4], P('segment'), may hold values from 266.043 to 1064.172
- adapt_down: bfloat16 [4, 12288, 64], P('segment', 'tensor'), may hold values from -0.0546875 to 0.0546875
- adapt_up: bfloat16 [4, 64, 12288], P('segment', None, 'tensor'), may hold values from -0.375 to 0.375
Outputs:
- grad_down: float32 [4, 12288, 64], P('segment', ('tensor', 'dp'))
- grad_up: float32 [4, 64, 12288], P('segment', None, ('tensor', 'dp'))
The draws below stay inside these ranges and needn't reach their ends.
Inputs may be any that keep to these rules, and one draw needn't show every extreme that they name: `lengths`: each example has at least one real row, and some example fills all 384 slots.
All inputs are finite; a program needn't handle non-finite values. No bound on the sum of `lengths` on one device may be relied on, other than what follows from the above.
Results may differ from the reference program's by a relative error of at most 0.011.
Values may be sent and summed in bfloat16 or wider, within the bound.
No kernel may reach another device: no remote copies, remote signals or barrier semaphores. Data moves between devices by JAX's collectives and lax.ppermute only.
A program may use at most 64 MiB of HBM per device.

```python
import math
import jax
import jax.numpy as jnp
import numpy as np
from jax import lax

D = 12288
R = 64
SEQ = 384
SEGMENTS = 4
EXAMPLES = 4


def draw_cotangent(key, part):
    key = jax.random.fold_in(key, 7)
    feature_ramp = jnp.arange(D, dtype=jnp.float32) / (D - 1)
    samples = jnp.clip(jax.random.normal(key, (EXAMPLES, SEQ, D), jnp.float32), -4.0, 4.0)
    scaling = 0.6 * jnp.power(3.0, feature_ramp)
    return (samples * scaling).astype(jnp.bfloat16)


def shard_levels(own_key, shape, shards, least, high):
    gain = 1.0
    for position, shards_of in shards:
        draws = jax.random.uniform(jax.random.fold_in(jax.random.fold_in(own_key, 6), position), (shards_of,), jnp.float32, least / len(shards), high / len(shards))
        gain = gain * jnp.repeat(jnp.exp(draws), shape[position] // shards_of).reshape((-1,) + (1,) * (len(shape) - 1 - position))
    return gain


def length_profile(count, total, most, slope):
    weights = [(1 << 20) // math.isqrt(grade ** slope) + 1 for grade in range(2, count + 1)]
    spare, holding = total - most - (count - 1), [1] * (count - 1)
    while spare > 0:
        movable = [i for i in range(count - 1) if holding[i] < most]
        pool, remaining = sum([weights[i] for i in movable]), spare
        for i in movable:
            addition = min(most - holding[i], max(1, remaining * weights[i] // pool), spare)
            holding[i] = holding[i] + addition
            spare = spare - addition
    return np.array([most] + holding)


def uneven(rng, count, total, reach, lean):
    if count == 2:
        one = jax.random.randint(rng, (), max(1, total - reach), min(reach, total - 1) + 1)
        return jnp.stack([one, total - one])
    sizes = jnp.asarray(length_profile(count, total, reach, lean), jnp.int32)
    twos = (count - 1) // 2
    giver, taker = sizes[1:1 + 2 * twos:2], sizes[2:2 + 2 * twos:2]
    margin = jnp.minimum(giver - 1, reach - taker)
    passed = jax.random.randint(jax.random.fold_in(rng, 1), (twos,), 0, 1 << 20) % (margin + 1)
    sizes = sizes.at[1:1 + 2 * twos:2].set(giver - passed).at[2:2 + 2 * twos:2].set(taker + passed)
    return sizes[jax.random.permutation(jax.random.fold_in(rng, 2), count)]


def noise(own_key, extent, scale, most, shards=(), held_as=jnp.bfloat16):
    level = shard_levels(own_key, extent, shards, -0.22, 0.18) if shards else 1.0
    values = jax.random.normal(own_key, extent, jnp.float32) * scale * level
    return jnp.minimum(jnp.maximum(values, -most), most).astype(held_as)


def setup_inputs(seed: int = 0) -> dict:
    arg_keys = jax.random.split(jax.random.key(seed), 7)
    return {
        "act_input": noise(arg_keys[0], (EXAMPLES, SEQ, D), 1.0, 6.0, ((0, 2), (2, 16))),
        "cotangent": draw_cotangent(jax.random.fold_in(arg_keys[6], 71), 0),
        "lengths": uneven(arg_keys[2], EXAMPLES, EXAMPLES * SEQ * 5 // 8, SEQ, 2).astype(jnp.int32),
        "clip_scale": jnp.clip(jnp.exp(math.log(1064.172) - 1.3862944 * jax.random.uniform(arg_keys[3], (SEGMENTS,), jnp.float32) ** shard_levels(arg_keys[3], (SEGMENTS,), ((0, 4),), -0.2, 0.2)), 266.043, 1064.172),
        "adapt_down": noise(arg_keys[4], (SEGMENTS, D, R), D ** -0.5, 0.0546875, ((0, 4), (1, 16))),
        "adapt_up": noise(arg_keys[5], (SEGMENTS, R, D), (4 * R) ** -0.5, 0.375, ((0, 4), (2, 16))),
    }


SLOPE_C = 0.7978845608
CUBIC = 0.044715

def gelu_value(values):
    tangent = jnp.tanh(SLOPE_C * (values + CUBIC * values * values * values))
    return 0.5 * values * (1.0 + tangent)

def gelu_slope(values):
    tangent = jnp.tanh(SLOPE_C * (values + CUBIC * values * values * values))
    return 0.5 * (1.0 + tangent) + 0.5 * values * (1.0 - tangent * tangent) * SLOPE_C * (1.0 + 3.0 * CUBIC * values * values)

def reference(act_input, cotangent, lengths, clip_scale, adapt_down, adapt_up):
    current = act_input
    stored = []
    for section in range(SEGMENTS):
        down_f = adapt_down[section].astype(jnp.float32)
        up_f = adapt_up[section].astype(jnp.float32)
        bottle = jnp.einsum('etd,dr->etr', current.astype(jnp.float32), down_f)
        hidden = gelu_value(bottle).astype(jnp.bfloat16)
        branch = jnp.einsum('etr,rd->etd', hidden.astype(jnp.float32), up_f)
        stored.append((current, bottle))
        current = (current.astype(jnp.float32) + branch).astype(jnp.bfloat16)
    live_rows = jnp.arange(SEQ, dtype=jnp.int32)[None, :] < lengths[:, None]
    incoming = jnp.where(live_rows[:, :, None], cotangent, jnp.zeros_like(cotangent))
    grads_down = []
    grads_up = []
    for section in reversed(range(SEGMENTS)):
        current, bottle = stored[section]
        down_f = adapt_down[section].astype(jnp.float32)
        up_f = adapt_up[section].astype(jnp.float32)
        hidden = gelu_value(bottle).astype(jnp.bfloat16)
        incoming_f = incoming.astype(jnp.float32)
        grad_up_each = jnp.einsum('etr,etd->erd', hidden.astype(jnp.float32), incoming_f)
        spread = jnp.einsum('etd,rd->etr', incoming_f, up_f)
        slope_grad = (spread * gelu_slope(bottle)).astype(jnp.bfloat16)
        slope_f = slope_grad.astype(jnp.float32)
        grad_down_each = jnp.einsum('etd,etr->edr', current.astype(jnp.float32), slope_f)
        backward = jnp.einsum('etr,dr->etd', slope_f, down_f)
        incoming = (incoming_f + backward).astype(jnp.bfloat16)
        squares = lax.optimization_barrier(jnp.sum(grad_down_each * grad_down_each, axis=(1, 2))) + lax.optimization_barrier(jnp.sum(grad_up_each * grad_up_each, axis=(1, 2)))
        factor = clip_scale[section] / (jnp.sqrt(squares) + 0.01)
        grads_down.append(lax.optimization_barrier(jnp.sum(factor[:, None, None] * grad_down_each, axis=0)))
        grads_up.append(lax.optimization_barrier(jnp.sum(factor[:, None, None] * grad_up_each, axis=0)))
    grad_down = jnp.stack(grads_down[::-1], axis=0)
    grad_up = jnp.stack(grads_up[::-1], axis=0)
    return (grad_down, grad_up)
```

```python
import jax
import jax.numpy as jnp
from jax import lax
from jax.sharding import PartitionSpec as P

SLOPE_C = 0.7978845608
CUBIC = 0.044715
BF = jnp.bfloat16
F32 = jnp.float32


def gelu_both(values):
    squared = values * values
    tangent = jnp.tanh(SLOPE_C * values * (1.0 + CUBIC * squared))
    value = 0.5 * values * (1.0 + tangent)
    slope = 0.5 * (1.0 + tangent) + 0.5 * values * (1.0 - tangent * tangent) * SLOPE_C * (
        1.0 + 3.0 * CUBIC * squared
    )
    return value, slope


def dot(a, b, ca, cb):
    return lax.dot_general(a, b, (((ca,), (cb,)), ((), ())), preferred_element_type=F32)


def shards(act_input, cotangent, lengths, clip_scale, adapt_down, adapt_up):
    layers = lax.axis_size("segment")
    cuts = lax.axis_size("tensor")
    seg = lax.axis_index("segment")
    core = lax.axis_index("dp")
    micro, slots, width = act_input.shape
    rank = adapt_down.shape[2]
    rows = micro * slots
    chunk = rows // cuts
    half = rank // 2
    down = adapt_down[0]
    up = adapt_up[0]
    down_t = down.T

    received = []
    for k in range(1, layers):
        dest = (seg + k) % layers
        message = jnp.where(dest > seg, up, down_t)
        received.append(
            lax.ppermute(message, "segment", [(i, (i + k) % layers) for i in range(layers)])
        )

    live = jnp.arange(slots, dtype=jnp.int32)[None, :] < lengths[:, None]
    masked = jnp.where(live[:, :, None], cotangent, jnp.zeros_like(cotangent))
    first = dot(act_input.reshape(rows, width), down, 1, 0)
    last = dot(masked.reshape(rows, width), up, 1, 1)
    partial = jnp.concatenate([first, last], axis=1).astype(BF).reshape(cuts, chunk, 2 * rank)
    parts = lax.all_to_all(partial, "tensor", 0, 0, tiled=True)
    summed = jnp.sum(parts.astype(F32), axis=0).astype(BF)

    grams = []
    for k in range(1, layers):
        lower = (seg - k) % layers < seg
        left = jnp.where(lower, received[k - 1][half:], up[:half])
        right = jnp.where(lower, down_t, received[k - 1])
        grams.append(dot(left, right, 1, 1))
    gram = jnp.concatenate(grams, axis=0).astype(BF)
    gram = jnp.concatenate([gram[:48], gram[48:]], axis=1)
    message = jnp.concatenate([summed, gram], axis=0)
    spread_out = jnp.broadcast_to(message[None], (layers * cuts,) + message.shape)
    gathered = lax.all_to_all(spread_out, ("segment", "tensor"), 0, 0, tiled=True)
    gathered = gathered.reshape(layers, cuts, chunk + 48, 2 * rank)
    both = gathered[:, :, :chunk].reshape(layers, rows, 2 * rank).astype(F32)
    packed = jnp.sum(gathered[:, :, chunk:].astype(F32), axis=1).astype(BF)
    packed = jnp.concatenate([packed[:, :, :rank], packed[:, :, rank:]], axis=1)

    def gram_of(i, j):
        a, b = (i - j) % layers - 1, (j - i) % layers - 1
        return jnp.concatenate(
            [packed[i, a * half : (a + 1) * half], packed[j, b * half : (b + 1) * half]], axis=0
        )

    hidden, slope_of = [], []
    for j in range(layers):
        bottle = both[j, :, :rank]
        for i in range(j):
            bottle = bottle + dot(hidden[i], gram_of(i, j), 1, 0)
        value, slope = gelu_both(bottle)
        hidden.append(value.astype(BF))
        slope_of.append(slope)
    slopes = [None] * layers
    for i in reversed(range(layers)):
        spread = both[i, :, rank:]
        for j in range(i + 1, layers):
            spread = spread + dot(slopes[j], gram_of(i, j), 1, 1)
        slopes[i] = (spread * slope_of[i]).astype(BF)

    hidden = jnp.stack(hidden).reshape(layers, micro, slots, rank)
    slopes = jnp.stack(slopes).reshape(layers, micro, slots, rank)
    mine_h = lax.dynamic_index_in_dim(hidden, seg, 0, keepdims=False)
    mine_s = lax.dynamic_index_in_dim(slopes, seg, 0, keepdims=False)

    up_each = jnp.einsum("etr,etd->erd", mine_h, masked, preferred_element_type=F32)
    down_each = jnp.einsum("etr,etd->erd", mine_s, act_input, preferred_element_type=F32)
    for k in range(1, layers):
        peer = (seg - k) % layers
        lower = peer < seg
        theirs_h = lax.dynamic_index_in_dim(hidden, peer, 0, keepdims=False)
        theirs_s = lax.dynamic_index_in_dim(slopes, peer, 0, keepdims=False)
        left = jnp.where(lower, mine_s, mine_h)
        right = jnp.where(lower, theirs_h, theirs_s)
        mix = jnp.einsum("etr,etq->erq", left, right, preferred_element_type=F32).astype(BF)
        extra = jnp.einsum("erq,qd->erd", mix, received[k - 1], preferred_element_type=F32)
        up_each = up_each + jnp.where(lower, 0.0, extra)
        down_each = down_each + jnp.where(lower, extra, 0.0)
    each = jnp.concatenate([down_each, up_each], axis=1)
    squares = jnp.sum(each * each, axis=(1, 2))

    cores = lax.axis_size("dp")
    local = width // cores
    theirs = lax.dynamic_slice_in_dim(each, (1 - core) * local, local, 2)
    ours = lax.dynamic_slice_in_dim(each, core * local, local, 2)
    swapped = lax.ppermute(theirs.astype(BF), "dp", [(i, 1 - i) for i in range(cores)])
    note = jnp.broadcast_to(jnp.repeat(squares, 64)[None], (cuts * cores, 128))
    notes = lax.all_to_all(note, ("tensor", "dp"), 0, 0, tiled=True)
    totals = jnp.sum(notes.reshape(cuts, cores, micro, 64), axis=0)[:, :, 0]
    factors = clip_scale[0] / (jnp.sqrt(totals) + 0.01)
    own = lax.dynamic_index_in_dim(factors, core, 0, keepdims=False)
    other = lax.dynamic_index_in_dim(factors, 1 - core, 0, keepdims=False)
    out = jnp.sum(own[:, None, None] * ours, axis=0) + jnp.sum(
        other[:, None, None] * swapped.astype(F32), axis=0
    )
    return (out[:rank].T[None], out[rank:][None])


def solution(mesh):
    return jax.shard_map(
        shards,
        mesh=mesh,
        in_specs=(
            P("dp", None, "tensor"),
            P("dp", None, "tensor"),
            P("dp"),
            P("segment"),
            P("segment", "tensor", None),
            P("segment", None, "tensor"),
        ),
        out_specs=(P("segment", ("tensor", "dp"), None), P("segment", None, ("tensor", "dp"))),
        check_vma=False,
    )
```

```python
import jax
import jax.numpy as jnp
from jax import lax
from jax.experimental import pallas as pl
from jax.experimental.pallas import tpu as pltpu
from jax.sharding import PartitionSpec as P

SLOPE_C = 0.7978845608
CUBIC = 0.044715
BF = jnp.bfloat16
F32 = jnp.float32
VMEM = pl.BlockSpec(memory_space=pltpu.VMEM)
SMEM = pl.BlockSpec(memory_space=pltpu.SMEM)
ANY = pl.BlockSpec(memory_space=pl.ANY)

LAYERS = 4
CUTS = 16
SLOTS = 384
WIDTH = 768
RANK = 64
HALF = RANK // 2
LANES = 2 * RANK
PIECE = SLOTS // CUTS
PACK = 48
LOCAL = WIDTH // 2


def dot(a, b, ca, cb):
    return lax.dot_general(a, b, (((ca,), (cb,)), ((), ())), preferred_element_type=F32)


def gelu_both(values):
    squared = values * values
    tangent = jnp.tanh(values * (SLOPE_C + SLOPE_C * CUBIC * squared))
    half = 0.5 + 0.5 * tangent
    slope = half + values * (0.5 - 0.5 * tangent * tangent) * (
        SLOPE_C + 3.0 * SLOPE_C * CUBIC * squared
    )
    return values * half, slope


PROJECT_STEPS = 2
PROJECT_ROWS = SLOTS // PROJECT_STEPS


def project_body(lengths, act, cot, down, up, out):
    base = pl.program_id(0) * PROJECT_ROWS
    rows = 2 * PROJECT_ROWS
    first = dot(act[...].reshape(rows, WIDTH), down[0], 1, 0)
    last = dot(cot[...].reshape(rows, WIDTH), up[0], 1, 1)
    first = jnp.concatenate([first[:PROJECT_ROWS], first[PROJECT_ROWS:]], axis=1)
    last = jnp.concatenate([last[:PROJECT_ROWS], last[PROJECT_ROWS:]], axis=1)
    slot = lax.broadcasted_iota(jnp.int32, (PROJECT_ROWS, LANES), 0) + base
    lane = lax.broadcasted_iota(jnp.int32, (PROJECT_ROWS, LANES), 1)
    last = jnp.where(slot < jnp.where(lane < RANK, lengths[0], lengths[1]), last, 0.0)
    for i in range(PROJECT_ROWS // PIECE):
        part = slice(i * PIECE, (i + 1) * PIECE)
        out[i] = jnp.concatenate([first[part], last[part]], axis=0).astype(BF)


def project(lengths, act, cot, down, up):
    block = pl.BlockSpec((2, PROJECT_ROWS, WIDTH), lambda i: (0, i, 0))
    return pl.pallas_call(
        project_body,
        grid=(PROJECT_STEPS,),
        in_specs=[
            SMEM,
            block,
            block,
            pl.BlockSpec((1, WIDTH, RANK), lambda i: (0, 0, 0)),
            pl.BlockSpec((1, RANK, WIDTH), lambda i: (0, 0, 0)),
        ],
        out_specs=pl.BlockSpec((CUTS // PROJECT_STEPS, 2 * PIECE, LANES), lambda i: (i, 0, 0)),
        out_shape=jax.ShapeDtypeStruct((CUTS, 2 * PIECE, LANES), BF),
        compiler_params=pltpu.CompilerParams(vmem_limit_bytes=16 << 20),
        cost_estimate=pl.CostEstimate(flops=150000000, bytes_accessed=2800000, transcendentals=0),
    )(lengths, act, cot, down, up)


def reduce_body(parts, up, down_t, one, two, three, out):
    seg = lax.axis_index("segment")
    total = parts[0].astype(F32)
    for i in range(1, CUTS):
        total = total + parts[i].astype(F32)
    pieces = []
    for k, other in ((1, one), (2, two), (3, three)):
        lower = seg >= k
        left = jnp.where(lower, other[HALF:], up[0, :HALF])
        right = jnp.where(lower, down_t[...], other[...])
        pieces.append(dot(left, right, 1, 1))
    grams = jnp.concatenate(pieces, axis=0)
    grams = jnp.concatenate([grams[:PACK], grams[PACK:]], axis=1)
    message = jnp.concatenate([total, grams], axis=0).astype(BF)
    for i in range(LAYERS * CUTS):
        out[i] = message


def reduce_parts(parts, up, down_t, peers):
    return pl.pallas_call(
        reduce_body,
        in_specs=[VMEM] * 6,
        out_specs=VMEM,
        out_shape=jax.ShapeDtypeStruct((LAYERS * CUTS, 2 * PIECE + PACK, LANES), BF),
        compiler_params=pltpu.CompilerParams(vmem_limit_bytes=16 << 20),
        cost_estimate=pl.CostEstimate(flops=10000000, bytes_accessed=2300000, transcendentals=0),
    )(parts, up, down_t, *peers)


def gradient_body(
    lengths, gathered, one, two, three, act_hbm, cot_hbm,
    theirs, ours, note,
    act, cot, first, last, hidden, slopes, steep, each, sems,
):
    seg = lax.axis_index("segment")
    core = lax.axis_index("dp")
    act_copy = pltpu.make_async_copy(act_hbm, act, sems.at[0])
    cot_copy = pltpu.make_async_copy(cot_hbm, cot, sems.at[1])
    act_copy.start()
    cot_copy.start()

    packed = []
    for layer in range(LAYERS):
        total = None
        for t in range(CUTS):
            at = layer * CUTS + t
            block = gathered[at, : 2 * PIECE].astype(F32)
            first[layer, t * PIECE : (t + 1) * PIECE] = block[:PIECE]
            last[layer, t * PIECE : (t + 1) * PIECE] = block[PIECE:]
            gram = gathered[at, 2 * PIECE :].astype(F32)
            total = gram if total is None else total + gram
        packed.append(jnp.concatenate([total[:, :RANK], total[:, RANK:]], axis=0))

    def gram_of(i, j):
        a, b = (i - j) % LAYERS - 1, (j - i) % LAYERS - 1
        gram = jnp.concatenate(
            [packed[i][a * HALF : (a + 1) * HALF], packed[j][b * HALF : (b + 1) * HALF]], axis=0
        )
        zero = jnp.zeros_like(gram)
        return jnp.concatenate(
            [jnp.concatenate([gram, zero], axis=1), jnp.concatenate([zero, gram], axis=1)], axis=0
        ).astype(BF)

    grams = {(i, j): gram_of(i, j) for j in range(LAYERS) for i in range(j)}

    for j in range(LAYERS):
        bottle = first[j]
        for i in range(j):
            bottle = bottle + dot(hidden[i], grams[i, j], 1, 0)
        value, slope = gelu_both(bottle)
        hidden[j] = value.astype(BF)
        steep[j] = slope
    for i in reversed(range(LAYERS)):
        spread = last[i]
        for j in range(i + 1, LAYERS):
            spread = spread + dot(slopes[j], grams[i, j], 1, 1)
        slopes[i] = (spread * steep[i]).astype(BF)

    slot = lax.broadcasted_iota(jnp.int32, (SLOTS, LANES), 0)
    lane = lax.broadcasted_iota(jnp.int32, (SLOTS, LANES), 1)
    live = slot < jnp.where(lane < RANK, lengths[0], lengths[1])
    mine_h = jnp.where(live, hidden[seg].astype(F32), 0.0).T.astype(BF)
    mine_s = slopes[seg].astype(F32).T.astype(BF)

    lefts = []
    for k in range(1, LAYERS):
        peer = lax.rem(seg + LAYERS - k, LAYERS)
        lower = seg >= k
        left = jnp.where(lower, mine_s, mine_h)
        right = jnp.where(lower, hidden[peer], slopes[peer])
        mix = dot(left, right, 1, 0)
        mix = jnp.concatenate([mix[:RANK, :RANK], mix[RANK:, RANK:]], axis=0)
        lefts.append(
            jnp.concatenate([jnp.where(lower, mix, 0.0), jnp.where(lower, 0.0, mix)], axis=0)
        )
    left = jnp.concatenate(lefts, axis=1).astype(BF)
    peers = jnp.concatenate([one[...], two[...], three[...]], axis=0)
    act_copy.wait()
    cot_copy.wait()
    each[...] = dot(left, peers, 1, 0)
    for e in range(2):
        rows = slice(e * RANK, (e + 1) * RANK)
        other = slice((2 + e) * RANK, (3 + e) * RANK)
        down_grad = each[rows] + dot(mine_s[rows], act[e], 1, 0)
        up_grad = each[other] + dot(mine_h[rows], cot[e], 1, 0)
        each[rows] = down_grad
        each[other] = up_grad
        square = jnp.sum(down_grad * down_grad + up_grad * up_grad)
        note[:, rows] = jnp.full((2 * CUTS, RANK), square, F32)
    keep = pl.multiple_of(core * LOCAL, 128)
    give = pl.multiple_of((1 - core) * LOCAL, 128)
    ours[...] = each[:, pl.ds(keep, LOCAL)]
    theirs[...] = each[:, pl.ds(give, LOCAL)].astype(BF)


def gradients(lengths, gathered, peers, act, cot):
    wide = (LAYERS, SLOTS, LANES)
    return pl.pallas_call(
        gradient_body,
        in_specs=[SMEM] + [VMEM] * 4 + [ANY] * 2,
        out_specs=[VMEM] * 3,
        out_shape=[
            jax.ShapeDtypeStruct((4 * RANK, LOCAL), BF),
            jax.ShapeDtypeStruct((4 * RANK, LOCAL), F32),
            jax.ShapeDtypeStruct((2 * CUTS, LANES), F32),
        ],
        scratch_shapes=[
            pltpu.VMEM((2, SLOTS, WIDTH), BF),
            pltpu.VMEM((2, SLOTS, WIDTH), BF),
            pltpu.VMEM(wide, F32),
            pltpu.VMEM(wide, F32),
            pltpu.VMEM(wide, BF),
            pltpu.VMEM(wide, BF),
            pltpu.VMEM(wide, F32),
            pltpu.VMEM((4 * RANK, WIDTH), F32),
            pltpu.SemaphoreType.DMA((2,)),
        ],
        compiler_params=pltpu.CompilerParams(vmem_limit_bytes=32 << 20),
        cost_estimate=pl.CostEstimate(
            flops=600000000, bytes_accessed=5000000, transcendentals=200000
        ),
    )(lengths, gathered, *peers, act, cot)


def scale_body(clip, notes, ours, swapped, out_down, out_up):
    core = lax.axis_index("dp")
    row = lax.broadcasted_iota(jnp.int32, (2 * CUTS, LANES), 0)
    is_own = lax.rem(row, 2) == core
    values = notes[...]

    def factors(picked):
        total = jnp.sum(jnp.where(picked, values, 0.0), axis=0, keepdims=True)
        return clip[0] / (jnp.sqrt(total) + 0.01)

    own = factors(is_own)
    other = factors(jnp.logical_not(is_own))

    def combined(start):
        total = None
        for e in range(2):
            rows = slice(start + e * RANK, start + (e + 1) * RANK)
            at = slice(e * RANK, e * RANK + 1)
            term = own[:, at] * ours[rows] + other[:, at] * swapped[rows].astype(F32)
            total = term if total is None else total + term
        return total

    out_down[0] = combined(0).T
    out_up[0] = combined(2 * RANK)


def scaled(clip, notes, ours, swapped):
    return pl.pallas_call(
        scale_body,
        in_specs=[SMEM] + [VMEM] * 3,
        out_specs=[VMEM] * 2,
        out_shape=[
            jax.ShapeDtypeStruct((1, LOCAL, RANK), F32),
            jax.ShapeDtypeStruct((1, RANK, LOCAL), F32),
        ],
        compiler_params=pltpu.CompilerParams(vmem_limit_bytes=16 << 20),
        cost_estimate=pl.CostEstimate(flops=300000, bytes_accessed=900000, transcendentals=0),
    )(clip, notes, ours, swapped)


def shards(act_input, cotangent, lengths, clip_scale, adapt_down, adapt_up):
    seg = lax.axis_index("segment")
    up = adapt_up[0]
    down_t = adapt_down[0].T
    peers = []
    for k in range(1, LAYERS):
        message = jnp.where(seg + k < LAYERS, up, down_t)
        peers.append(
            lax.ppermute(message, "segment", [(i, (i + k) % LAYERS) for i in range(LAYERS)])
        )
    partial = project(lengths, act_input, cotangent, adapt_down, adapt_up)
    parts = lax.all_to_all(partial, "tensor", 0, 0, tiled=True)
    message = reduce_parts(parts, adapt_up, down_t, peers)
    gathered = lax.all_to_all(message, ("segment", "tensor"), 0, 0, tiled=True)
    theirs, ours, note = gradients(lengths, gathered, peers, act_input, cotangent)
    swapped = lax.ppermute(theirs, "dp", [(0, 1), (1, 0)])
    notes = lax.all_to_all(note, ("tensor", "dp"), 0, 0, tiled=True)
    return scaled(clip_scale, notes, ours, swapped)


def solution(mesh):
    return jax.shard_map(
        shards,
        mesh=mesh,
        in_specs=(
            P("dp", None, "tensor"),
            P("dp", None, "tensor"),
            P("dp"),
            P("segment"),
            P("segment", "tensor", None),
            P("segment", None, "tensor"),
        ),
        out_specs=(P("segment", ("tensor", "dp"), None), P("segment", None, ("tensor", "dp"))),
        check_vma=False,
    )
```

```python
import jax
import jax.numpy as jnp
from jax import lax
from jax.experimental import pallas as pl
from jax.experimental.pallas import tpu as pltpu
from jax.sharding import PartitionSpec as P

SLOPE_C = 0.7978845608
CUBIC = 0.044715
BF = jnp.bfloat16
F32 = jnp.float32
VMEM = pl.BlockSpec(memory_space=pltpu.VMEM)
SMEM = pl.BlockSpec(memory_space=pltpu.SMEM)
HBM = pl.BlockSpec(memory_space=pltpu.HBM)

LAYERS = 4
CUTS = 16
SLOTS = 384
WIDTH = 768
RANK = 64
HALF = RANK // 2
LANES = 2 * RANK
PIECE = SLOTS // CUTS
EXTRA = 16
LOCAL = WIDTH // 2


def dot(a, b, ca, cb):
    return lax.dot_general(a, b, (((ca,), (cb,)), ((), ())), preferred_element_type=F32)


def gelu_both(values):
    squared = values * values
    tangent = jnp.tanh(values * (SLOPE_C + SLOPE_C * CUBIC * squared))
    half = 0.5 + 0.5 * tangent
    slope = half + values * (0.5 - 0.5 * tangent * tangent) * (
        SLOPE_C + 3.0 * SLOPE_C * CUBIC * squared
    )
    return values * half, slope


STEPS = 4
STEP_ROWS = SLOTS // STEPS


def project_body(act_hbm, cot_hbm, down_t, up, out, act, cot, sems):
    copies = []
    for i in range(STEPS):
        rows = pl.ds(i * STEP_ROWS, STEP_ROWS)
        pair = []
        for j, (source, target) in enumerate(((act_hbm, act), (cot_hbm, cot))):
            copy = pltpu.make_async_copy(source.at[:, rows], target.at[:, rows], sems.at[i, j])
            copy.start()
            pair.append(copy)
        copies.append(pair)
    for i in range(STEPS):
        rows = pl.ds(i * STEP_ROWS, STEP_ROWS)
        copies[i][0].wait()
        first = dot(act[:, rows].reshape(2 * STEP_ROWS, WIDTH), down_t[...], 1, 1)
        copies[i][1].wait()
        last = dot(cot[:, rows].reshape(2 * STEP_ROWS, WIDTH), up[0], 1, 1)
        first = jnp.concatenate([first[:STEP_ROWS], first[STEP_ROWS:]], axis=1)
        last = jnp.concatenate([last[:STEP_ROWS], last[STEP_ROWS:]], axis=1)
        for j in range(STEP_ROWS // PIECE):
            part = slice(j * PIECE, (j + 1) * PIECE)
            out[i * (STEP_ROWS // PIECE) + j] = jnp.concatenate(
                [first[part], last[part]], axis=0
            ).astype(BF)


def project(act, cot, down_t, up):
    return pl.pallas_call(
        project_body,
        in_specs=[HBM, HBM, VMEM, VMEM],
        out_specs=VMEM,
        out_shape=jax.ShapeDtypeStruct((CUTS, 2 * PIECE, LANES), BF),
        scratch_shapes=[
            pltpu.VMEM((2, SLOTS, WIDTH), BF),
            pltpu.VMEM((2, SLOTS, WIDTH), BF),
            pltpu.SemaphoreType.DMA((STEPS, 2)),
        ],
        compiler_params=pltpu.CompilerParams(vmem_limit_bytes=16 << 20),
        cost_estimate=pl.CostEstimate(flops=150000000, bytes_accessed=2800000, transcendentals=0),
    )(act, cot, down_t, up)


def weave_body(partial, up, down_t, one, two, three, out):
    seg = lax.axis_index("segment")
    for k, other in ((1, one), (2, two), (3, three)):
        lower = seg >= k
        left = jnp.where(lower, other[HALF:], up[0, :HALF])
        right = jnp.where(lower, down_t[...], other[...])
        gram = dot(left, right, 1, 1)
        gram = jnp.concatenate([gram, jnp.zeros_like(gram)], axis=1)
        for q in range(4):
            tile = gram[q * 8 : (q + 1) * 8]
            out[(k - 1) * 4 + q, 2 * PIECE :] = jnp.concatenate(
                [tile, jnp.zeros_like(tile)], axis=0
            ).astype(BF)
    for t in range(CUTS):
        out[t, : 2 * PIECE] = partial[t]
    for t in range(12, CUTS):
        out[t, 2 * PIECE :] = jnp.zeros((EXTRA, LANES), BF)


def weave(partial, up, down_t, peers):
    return pl.pallas_call(
        weave_body,
        in_specs=[VMEM] * 6,
        out_specs=VMEM,
        out_shape=jax.ShapeDtypeStruct((CUTS, 2 * PIECE + EXTRA, LANES), BF),
        compiler_params=pltpu.CompilerParams(vmem_limit_bytes=16 << 20),
        cost_estimate=pl.CostEstimate(flops=10000000, bytes_accessed=1000000, transcendentals=0),
    )(partial, up, down_t, *peers)


def reduce_body(lengths, parts, out):
    base = lax.axis_index("tensor") * PIECE
    total = parts[0].astype(F32)
    for i in range(1, CUTS):
        total = total + parts[i].astype(F32)
    slot = lax.broadcasted_iota(jnp.int32, (PIECE, LANES), 0) + base
    lane = lax.broadcasted_iota(jnp.int32, (PIECE, LANES), 1)
    live = slot < jnp.where(lane < RANK, lengths[0], lengths[1])
    last = jnp.where(live, total[PIECE : 2 * PIECE], 0.0)
    message = jnp.concatenate([total[:PIECE], last, total[2 * PIECE :]], axis=0).astype(BF)
    for i in range(LAYERS * CUTS):
        out[i] = message


def reduce_parts(lengths, parts):
    return pl.pallas_call(
        reduce_body,
        in_specs=[SMEM, VMEM],
        out_specs=VMEM,
        out_shape=jax.ShapeDtypeStruct((LAYERS * CUTS, 2 * PIECE + EXTRA, LANES), BF),
        compiler_params=pltpu.CompilerParams(vmem_limit_bytes=16 << 20),
        cost_estimate=pl.CostEstimate(flops=200000, bytes_accessed=1300000, transcendentals=0),
    )(lengths, parts)


def gradient_body(
    lengths, gathered, one, two, three, act_hbm, cot_hbm,
    theirs, ours, note,
    act, cot, first, last, hidden, slopes, steep, each, sems,
):
    seg = lax.axis_index("segment")
    core = lax.axis_index("dp")
    act_copy = pltpu.make_async_copy(act_hbm, act, sems.at[0])
    cot_copy = pltpu.make_async_copy(cot_hbm, cot, sems.at[1])
    act_copy.start()
    cot_copy.start()

    packed = []
    for layer in range(LAYERS):
        tiles = []
        for t in range(CUTS):
            block = gathered[layer * CUTS + t].astype(F32)
            first[layer, t * PIECE : (t + 1) * PIECE] = block[:PIECE]
            last[layer, t * PIECE : (t + 1) * PIECE] = block[PIECE : 2 * PIECE]
            if t < 12:
                tiles.append(block[2 * PIECE : 2 * PIECE + 8, :RANK])
        packed.append(jnp.concatenate(tiles, axis=0))

    def gram_of(i, j):
        a, b = (i - j) % LAYERS - 1, (j - i) % LAYERS - 1
        gram = jnp.concatenate(
            [packed[i][a * HALF : (a + 1) * HALF], packed[j][b * HALF : (b + 1) * HALF]], axis=0
        )
        zero = jnp.zeros_like(gram)
        return jnp.concatenate(
            [jnp.concatenate([gram, zero], axis=1), jnp.concatenate([zero, gram], axis=1)], axis=0
        ).astype(BF)

    grams = {(i, j): gram_of(i, j) for j in range(LAYERS) for i in range(j)}

    for j in range(LAYERS):
        bottle = first[j]
        for i in range(j):
            bottle = bottle + dot(hidden[i], grams[i, j], 1, 0)
        value, slope = gelu_both(bottle)
        hidden[j] = value.astype(BF)
        steep[j] = slope
    for i in reversed(range(LAYERS)):
        spread = last[i]
        for j in range(i + 1, LAYERS):
            spread = spread + dot(slopes[j], grams[i, j], 1, 1)
        slopes[i] = (spread * steep[i]).astype(BF)

    slot = lax.broadcasted_iota(jnp.int32, (SLOTS, LANES), 0)
    lane = lax.broadcasted_iota(jnp.int32, (SLOTS, LANES), 1)
    live = slot < jnp.where(lane < RANK, lengths[0], lengths[1])
    mine_h = jnp.where(live, hidden[seg].astype(F32), 0.0).T.astype(BF)
    mine_s = slopes[seg].astype(F32).T.astype(BF)

    lefts = []
    for k in range(1, LAYERS):
        peer = lax.rem(seg + LAYERS - k, LAYERS)
        lower = seg >= k
        left = jnp.where(lower, mine_s, mine_h)
        right = jnp.where(lower, hidden[peer], slopes[peer])
        mix = dot(left, right, 1, 0)
        mix = jnp.concatenate([mix[:RANK, :RANK], mix[RANK:, RANK:]], axis=0)
        lefts.append(
            jnp.concatenate([jnp.where(lower, mix, 0.0), jnp.where(lower, 0.0, mix)], axis=0)
        )
    left = jnp.concatenate(lefts, axis=1).astype(BF)
    peers = jnp.concatenate([one[...], two[...], three[...]], axis=0)
    act_copy.wait()
    cot_copy.wait()
    each[...] = dot(left, peers, 1, 0)
    for e in range(2):
        rows = slice(e * RANK, (e + 1) * RANK)
        other = slice((2 + e) * RANK, (3 + e) * RANK)
        down_grad = each[rows] + dot(mine_s[rows], act[e], 1, 0)
        up_grad = each[other] + dot(mine_h[rows], cot[e], 1, 0)
        each[rows] = down_grad
        each[other] = up_grad
        square = jnp.sum(down_grad * down_grad + up_grad * up_grad)
        note[:, rows] = jnp.full((2 * CUTS, RANK), square, F32)
    keep = pl.multiple_of(core * LOCAL, 128)
    give = pl.multiple_of((1 - core) * LOCAL, 128)
    ours[...] = each[:, pl.ds(keep, LOCAL)]
    theirs[...] = each[:, pl.ds(give, LOCAL)].astype(BF)


def gradients(lengths, gathered, peers, act, cot):
    wide = (LAYERS, SLOTS, LANES)
    return pl.pallas_call(
        gradient_body,
        in_specs=[SMEM] + [VMEM] * 4 + [HBM] * 2,
        out_specs=[VMEM] * 3,
        out_shape=[
            jax.ShapeDtypeStruct((4 * RANK, LOCAL), BF),
            jax.ShapeDtypeStruct((4 * RANK, LOCAL), F32),
            jax.ShapeDtypeStruct((2 * CUTS, LANES), F32),
        ],
        scratch_shapes=[
            pltpu.VMEM((2, SLOTS, WIDTH), BF),
            pltpu.VMEM((2, SLOTS, WIDTH), BF),
            pltpu.VMEM(wide, F32),
            pltpu.VMEM(wide, F32),
            pltpu.VMEM(wide, BF),
            pltpu.VMEM(wide, BF),
            pltpu.VMEM(wide, F32),
            pltpu.VMEM((4 * RANK, WIDTH), F32),
            pltpu.SemaphoreType.DMA((2,)),
        ],
        compiler_params=pltpu.CompilerParams(vmem_limit_bytes=32 << 20),
        cost_estimate=pl.CostEstimate(
            flops=600000000, bytes_accessed=5000000, transcendentals=200000
        ),
    )(lengths, gathered, *peers, act, cot)


def scale_body(clip, notes, ours, swapped, out_down, out_up):
    core = lax.axis_index("dp")
    row = lax.broadcasted_iota(jnp.int32, (2 * CUTS, LANES), 0)
    is_own = lax.rem(row, 2) == core
    values = notes[...]

    def factors(picked):
        total = jnp.sum(jnp.where(picked, values, 0.0), axis=0, keepdims=True)
        return clip[0] / (jnp.sqrt(total) + 0.01)

    own = factors(is_own)
    other = factors(jnp.logical_not(is_own))

    def combined(start):
        total = None
        for e in range(2):
            rows = slice(start + e * RANK, start + (e + 1) * RANK)
            at = slice(e * RANK, e * RANK + 1)
            term = own[:, at] * ours[rows] + other[:, at] * swapped[rows].astype(F32)
            total = term if total is None else total + term
        return total

    out_down[0] = combined(0)
    out_up[0] = combined(2 * RANK)


def scaled(clip, notes, ours, swapped):
    return pl.pallas_call(
        scale_body,
        in_specs=[SMEM] + [VMEM] * 3,
        out_specs=[VMEM] * 2,
        out_shape=[
            jax.ShapeDtypeStruct((1, RANK, LOCAL), F32),
            jax.ShapeDtypeStruct((1, RANK, LOCAL), F32),
        ],
        compiler_params=pltpu.CompilerParams(vmem_limit_bytes=16 << 20),
        cost_estimate=pl.CostEstimate(flops=300000, bytes_accessed=900000, transcendentals=0),
    )(clip, notes, ours, swapped)


def shards(act_input, cotangent, lengths, clip_scale, adapt_down, adapt_up):
    seg = lax.axis_index("segment")
    up = adapt_up[0]
    down_t = adapt_down[0].T
    peers = []
    for k in range(1, LAYERS):
        message = jnp.where(seg + k < LAYERS, up, down_t)
        peers.append(
            lax.ppermute(message, "segment", [(i, (i + k) % LAYERS) for i in range(LAYERS)])
        )
    partial = project(act_input, cotangent, down_t, adapt_up)
    woven = weave(partial, adapt_up, down_t, peers)
    parts = lax.all_to_all(woven, "tensor", 0, 0, tiled=True)
    message = reduce_parts(lengths, parts)
    gathered = lax.all_to_all(message, ("segment", "tensor"), 0, 0, tiled=True)
    theirs, ours, note = gradients(lengths, gathered, peers, act_input, cotangent)
    swapped = lax.ppermute(theirs, "dp", [(0, 1), (1, 0)])
    notes = lax.all_to_all(note, ("tensor", "dp"), 0, 0, tiled=True)
    grad_down, grad_up = scaled(clip_scale, notes, ours, swapped)
    return jnp.swapaxes(grad_down, 1, 2), grad_up


def solution(mesh):
    return jax.shard_map(
        shards,
        mesh=mesh,
        in_specs=(
            P("dp", None, "tensor"),
            P("dp", None, "tensor"),
            P("dp"),
            P("segment"),
            P("segment", "tensor", None),
            P("segment", None, "tensor"),
        ),
        out_specs=(P("segment", ("tensor", "dp"), None), P("segment", None, ("tensor", "dp"))),
        check_vma=False,
    )
```

```python
import jax
import jax.numpy as jnp
from jax import lax
from jax.experimental import pallas as pl
from jax.experimental.pallas import tpu as pltpu
from jax.sharding import PartitionSpec as P

SLOPE_C = 0.7978845608
CUBIC = 0.044715
BF = jnp.bfloat16
F32 = jnp.float32
VMEM = pl.BlockSpec(memory_space=pltpu.VMEM)
SMEM = pl.BlockSpec(memory_space=pltpu.SMEM)
HBM = pl.BlockSpec(memory_space=pltpu.HBM)

LAYERS = 4
CUTS = 16
SLOTS = 384
WIDTH = 768
RANK = 64
HALF = RANK // 2
LANES = 2 * RANK
PIECE = SLOTS // CUTS
EXTRA = 16
LOCAL = WIDTH // 2


def dot(a, b, ca, cb):
    return lax.dot_general(a, b, (((ca,), (cb,)), ((), ())), preferred_element_type=F32)


def gelu_both(values):
    squared = values * values
    tangent = jnp.tanh(values * (SLOPE_C + SLOPE_C * CUBIC * squared))
    half = 0.5 + 0.5 * tangent
    slope = half + values * (0.5 - 0.5 * tangent * tangent) * (
        SLOPE_C + 3.0 * SLOPE_C * CUBIC * squared
    )
    return values * half, slope


STEPS = 2
STEP_ROWS = SLOTS // STEPS


def project_body(act_hbm, cot_hbm, sent, kept, out, act, cot, sems):
    copies = []
    for i in range(STEPS):
        rows = pl.ds(i * STEP_ROWS, STEP_ROWS)
        pair = []
        for j, (source, target) in enumerate(((act_hbm, act), (cot_hbm, cot))):
            copy = pltpu.make_async_copy(source.at[:, rows], target.at[:, rows], sems.at[i, j])
            copy.start()
            pair.append(copy)
        copies.append(pair)
    final = lax.axis_index("segment") == LAYERS - 1
    down = jnp.where(final, sent[...], kept[...]).T
    up_t = jnp.where(final, kept[...], sent[...]).T
    for i in range(STEPS):
        rows = pl.ds(i * STEP_ROWS, STEP_ROWS)
        copies[i][0].wait()
        first = jnp.concatenate([dot(act[e, rows], down, 1, 0) for e in range(2)], axis=1)
        copies[i][1].wait()
        last = jnp.concatenate([dot(cot[e, rows], up_t, 1, 0) for e in range(2)], axis=1)
        for j in range(STEP_ROWS // PIECE):
            part = slice(j * PIECE, (j + 1) * PIECE)
            out[i * (STEP_ROWS // PIECE) + j] = jnp.concatenate(
                [first[part], last[part]], axis=0
            ).astype(BF)


def project(act, cot, sent, kept):
    return pl.pallas_call(
        project_body,
        in_specs=[HBM, HBM, VMEM, VMEM],
        out_specs=VMEM,
        out_shape=jax.ShapeDtypeStruct((CUTS, 2 * PIECE, LANES), BF),
        scratch_shapes=[
            pltpu.VMEM((2, SLOTS, WIDTH), BF),
            pltpu.VMEM((2, SLOTS, WIDTH), BF),
            pltpu.SemaphoreType.DMA((STEPS, 2)),
        ],
        compiler_params=pltpu.CompilerParams(vmem_limit_bytes=53 << 20),
        cost_estimate=pl.CostEstimate(flops=150000000, bytes_accessed=2800000, transcendentals=0),
    )(act, cot, sent, kept)


def weave_body(partial, to_one, to_two, to_three, one, two, three, out):
    seg = lax.axis_index("segment")
    for k, own, other in ((1, to_three, one), (2, to_two, two), (3, to_one, three)):
        lower = seg >= k
        left = jnp.where(lower, other[HALF:], own[:HALF])
        right = jnp.where(lower, own[...], other[...])
        gram = dot(left, right, 1, 1)
        gram = jnp.concatenate([gram, jnp.zeros_like(gram)], axis=1)
        for q in range(4):
            tile = gram[q * 8 : (q + 1) * 8]
            out[(k - 1) * 4 + q, 2 * PIECE :] = jnp.concatenate(
                [tile, jnp.zeros_like(tile)], axis=0
            ).astype(BF)
    for t in range(CUTS):
        out[t, : 2 * PIECE] = partial[t]
    for t in range(12, CUTS):
        out[t, 2 * PIECE :] = jnp.zeros((EXTRA, LANES), BF)


def weave(partial, messages, peers):
    return pl.pallas_call(
        weave_body,
        in_specs=[VMEM] * 7,
        out_specs=VMEM,
        out_shape=jax.ShapeDtypeStruct((CUTS, 2 * PIECE + EXTRA, LANES), BF),
        compiler_params=pltpu.CompilerParams(vmem_limit_bytes=16 << 20),
        cost_estimate=pl.CostEstimate(flops=10000000, bytes_accessed=1000000, transcendentals=0),
    )(partial, *messages, *peers)


def reduce_body(lengths, parts, out):
    base = lax.axis_index("tensor") * PIECE
    total = parts[0].astype(F32)
    for i in range(1, CUTS):
        total = total + parts[i].astype(F32)
    slot = lax.broadcasted_iota(jnp.int32, (PIECE, LANES), 0) + base
    lane = lax.broadcasted_iota(jnp.int32, (PIECE, LANES), 1)
    live = slot < jnp.where(lane < RANK, lengths[0], lengths[1])
    last = jnp.where(live, total[PIECE : 2 * PIECE], 0.0)
    message = jnp.concatenate([total[:PIECE], last, total[2 * PIECE :]], axis=0).astype(BF)
    for i in range(LAYERS * CUTS):
        out[i] = message


def reduce_parts(lengths, parts):
    return pl.pallas_call(
        reduce_body,
        in_specs=[SMEM, VMEM],
        out_specs=VMEM,
        out_shape=jax.ShapeDtypeStruct((LAYERS * CUTS, 2 * PIECE + EXTRA, LANES), BF),
        compiler_params=pltpu.CompilerParams(vmem_limit_bytes=16 << 20),
        cost_estimate=pl.CostEstimate(flops=200000, bytes_accessed=1300000, transcendentals=0),
    )(lengths, parts)


def gradient_body(
    lengths, gathered, one, two, three, act_hbm, cot_hbm,
    each, note,
    act, cot, first, last, hidden, slopes, steep, sems,
):
    seg = lax.axis_index("segment")
    act_copy = pltpu.make_async_copy(act_hbm, act, sems.at[0])
    cot_copy = pltpu.make_async_copy(cot_hbm, cot, sems.at[1])
    act_copy.start()
    cot_copy.start()

    packed = []
    for layer in range(LAYERS):
        tiles = []
        for t in range(CUTS):
            block = gathered[layer * CUTS + t].astype(F32)
            first[layer, t * PIECE : (t + 1) * PIECE] = block[:PIECE]
            last[layer, t * PIECE : (t + 1) * PIECE] = block[PIECE : 2 * PIECE]
            if t < 12:
                tiles.append(block[2 * PIECE : 2 * PIECE + 8, :RANK])
        packed.append(jnp.concatenate(tiles, axis=0))

    def gram_of(i, j):
        a, b = (i - j) % LAYERS - 1, (j - i) % LAYERS - 1
        gram = jnp.concatenate(
            [packed[i][a * HALF : (a + 1) * HALF], packed[j][b * HALF : (b + 1) * HALF]], axis=0
        )
        zero = jnp.zeros_like(gram)
        return jnp.concatenate(
            [jnp.concatenate([gram, zero], axis=1), jnp.concatenate([zero, gram], axis=1)], axis=0
        ).astype(BF)

    grams = {(i, j): gram_of(i, j) for j in range(LAYERS) for i in range(j)}

    for j in range(LAYERS):
        bottle = first[j]
        for i in range(j):
            bottle = bottle + dot(hidden[i], grams[i, j], 1, 0)
        value, slope = gelu_both(bottle)
        hidden[j] = value.astype(BF)
        steep[j] = slope
    for i in reversed(range(LAYERS)):
        spread = last[i]
        for j in range(i + 1, LAYERS):
            spread = spread + dot(slopes[j], grams[i, j], 1, 1)
        slopes[i] = (spread * steep[i]).astype(BF)

    slot = lax.broadcasted_iota(jnp.int32, (SLOTS, LANES), 0)
    lane = lax.broadcasted_iota(jnp.int32, (SLOTS, LANES), 1)
    live = slot < jnp.where(lane < RANK, lengths[0], lengths[1])
    mine_h = jnp.where(live, hidden[seg].astype(F32), 0.0).T.astype(BF)
    mine_s = slopes[seg].astype(F32).T.astype(BF)

    lefts = []
    for k in range(1, LAYERS):
        peer = lax.rem(seg + LAYERS - k, LAYERS)
        lower = seg >= k
        left = jnp.where(lower, mine_s, mine_h)
        right = jnp.where(lower, hidden[peer], slopes[peer])
        mix = dot(left, right, 1, 0)
        mix = jnp.concatenate([mix[:RANK, :RANK], mix[RANK:, RANK:]], axis=0)
        lefts.append(
            jnp.concatenate([jnp.where(lower, mix, 0.0), jnp.where(lower, 0.0, mix)], axis=0)
        )
    left = jnp.concatenate(lefts, axis=1).astype(BF)
    peers = jnp.concatenate([one[...], two[...], three[...]], axis=0)
    act_copy.wait()
    cot_copy.wait()
    each[...] = dot(left, peers, 1, 0)
    for e in range(2):
        rows = slice(e * RANK, (e + 1) * RANK)
        other = slice((2 + e) * RANK, (3 + e) * RANK)
        down_grad = each[rows] + dot(mine_s[rows], act[e], 1, 0)
        up_grad = each[other] + dot(mine_h[rows], cot[e], 1, 0)
        each[rows] = down_grad
        each[other] = up_grad
        square = jnp.sum(down_grad * down_grad + up_grad * up_grad)
        note[:, rows] = jnp.full((2 * CUTS, RANK), square, F32)


def gradients(lengths, gathered, peers, act, cot):
    wide = (LAYERS, SLOTS, LANES)
    return pl.pallas_call(
        gradient_body,
        in_specs=[SMEM] + [VMEM] * 4 + [HBM] * 2,
        out_specs=[VMEM] * 2,
        out_shape=[
            jax.ShapeDtypeStruct((4 * RANK, WIDTH), F32),
            jax.ShapeDtypeStruct((2 * CUTS, LANES), F32),
        ],
        scratch_shapes=[
            pltpu.VMEM((2, SLOTS, WIDTH), BF),
            pltpu.VMEM((2, SLOTS, WIDTH), BF),
            pltpu.VMEM(wide, F32),
            pltpu.VMEM(wide, F32),
            pltpu.VMEM(wide, BF),
            pltpu.VMEM(wide, BF),
            pltpu.VMEM(wide, F32),
            pltpu.SemaphoreType.DMA((2,)),
        ],
        compiler_params=pltpu.CompilerParams(vmem_limit_bytes=32 << 20),
        cost_estimate=pl.CostEstimate(
            flops=600000000, bytes_accessed=5000000, transcendentals=200000
        ),
    )(lengths, gathered, *peers, act, cot)


def share_body(each, theirs):
    give = pl.multiple_of((1 - lax.axis_index("dp")) * LOCAL, 128)
    theirs[...] = each[:, pl.ds(give, LOCAL)].astype(BF)


def share(each):
    return pl.pallas_call(
        share_body,
        in_specs=[VMEM],
        out_specs=VMEM,
        out_shape=jax.ShapeDtypeStruct((4 * RANK, LOCAL), BF),
        compiler_params=pltpu.CompilerParams(vmem_limit_bytes=16 << 20),
        cost_estimate=pl.CostEstimate(flops=100000, bytes_accessed=1000000, transcendentals=0),
    )(each)


def scale_body(clip, notes, each, swapped, out_down, out_up):
    core = lax.axis_index("dp")
    ours = each.at[:, pl.ds(pl.multiple_of(core * LOCAL, 128), LOCAL)]
    row = lax.broadcasted_iota(jnp.int32, (2 * CUTS, LANES), 0)
    is_own = lax.rem(row, 2) == core
    values = notes[...]

    def factors(picked):
        total = jnp.sum(jnp.where(picked, values, 0.0), axis=0, keepdims=True)
        return clip[0] / (jnp.sqrt(total) + 0.01)

    own = factors(is_own)
    other = factors(jnp.logical_not(is_own))

    def combined(start):
        total = None
        for e in range(2):
            rows = slice(start + e * RANK, start + (e + 1) * RANK)
            at = slice(e * RANK, e * RANK + 1)
            term = own[:, at] * ours[rows] + other[:, at] * swapped[rows].astype(F32)
            total = term if total is None else total + term
        return total

    out_down[0] = combined(0)
    out_up[0] = combined(2 * RANK)


def scaled(clip, notes, each, swapped):
    return pl.pallas_call(
        scale_body,
        in_specs=[SMEM] + [VMEM] * 3,
        out_specs=[VMEM] * 2,
        out_shape=[
            jax.ShapeDtypeStruct((1, RANK, LOCAL), F32),
            jax.ShapeDtypeStruct((1, RANK, LOCAL), F32),
        ],
        compiler_params=pltpu.CompilerParams(vmem_limit_bytes=16 << 20),
        cost_estimate=pl.CostEstimate(flops=300000, bytes_accessed=900000, transcendentals=0),
    )(clip, notes, each, swapped)


def shards(act_input, cotangent, lengths, clip_scale, adapt_down, adapt_up):
    seg = lax.axis_index("segment")
    up = adapt_up[0]
    down_t = adapt_down[0].T
    messages = [jnp.where(seg + k < LAYERS, up, down_t) for k in range(1, LAYERS)]
    peers = [
        lax.ppermute(messages[k - 1], "segment", [(i, (i + k) % LAYERS) for i in range(LAYERS)])
        for k in range(1, LAYERS)
    ]
    partial = project(act_input, cotangent, messages[0], jnp.where(seg + 1 < LAYERS, down_t, up))
    woven = weave(partial, messages, peers)
    parts = lax.all_to_all(woven, "tensor", 0, 0, tiled=True)
    message = reduce_parts(lengths, parts)
    gathered = lax.all_to_all(message, ("segment", "tensor"), 0, 0, tiled=True)
    each, note = gradients(lengths, gathered, peers, act_input, cotangent)
    swapped = lax.ppermute(share(each), "dp", [(0, 1), (1, 0)])
    notes = lax.all_to_all(note, ("tensor", "dp"), 0, 0, tiled=True)
    grad_down, grad_up = scaled(clip_scale, notes, each, swapped)
    return jnp.swapaxes(grad_down, 1, 2), grad_up


def solution(mesh):
    return jax.shard_map(
        shards,
        mesh=mesh,
        in_specs=(
            P("dp", None, "tensor"),
            P("dp", None, "tensor"),
            P("dp"),
            P("segment"),
            P("segment", "tensor", None),
            P("segment", None, "tensor"),
        ),
        out_specs=(P("segment", ("tensor", "dp"), None), P("segment", None, ("tensor", "dp"))),
        check_vma=False,
    )
```

```python
import jax
import jax.numpy as jnp
from jax import lax
from jax.experimental import pallas as pl
from jax.experimental.pallas import tpu as pltpu
from jax.sharding import PartitionSpec as P

SLOPE_C = 0.7978845608
CUBIC = 0.044715
BF = jnp.bfloat16
F32 = jnp.float32
VMEM = pl.BlockSpec(memory_space=pltpu.VMEM)
SMEM = pl.BlockSpec(memory_space=pltpu.SMEM)
HBM = pl.BlockSpec(memory_space=pltpu.HBM)

LAYERS = 4
CUTS = 16
SLOTS = 384
WIDTH = 768
RANK = 64
HALF = RANK // 2
LANES = 2 * RANK
PIECE = SLOTS // CUTS
EXTRA = 16
LOCAL = WIDTH // 2


def dot(a, b, ca, cb):
    return lax.dot_general(a, b, (((ca,), (cb,)), ((), ())), preferred_element_type=F32)


def gelu_both(values):
    squared = values * values
    tangent = jnp.tanh(values * (SLOPE_C + SLOPE_C * CUBIC * squared))
    half = 0.5 + 0.5 * tangent
    slope = half + values * (0.5 - 0.5 * tangent * tangent) * (
        SLOPE_C + 3.0 * SLOPE_C * CUBIC * squared
    )
    return values * half, slope


STEPS = 2
STEP_ROWS = SLOTS // STEPS


def project_body(
    lengths, clip, act_hbm, cot_hbm, sent, kept, out, limits, bounds, act, cot, sems
):
    copies = []
    for i in range(STEPS):
        rows = pl.ds(i * STEP_ROWS, STEP_ROWS)
        pair = []
        for j, (source, target) in enumerate(((act_hbm, act), (cot_hbm, cot))):
            copy = pltpu.make_async_copy(source.at[:, rows], target.at[:, rows], sems.at[i, j])
            copy.start()
            pair.append(copy)
        copies.append(pair)
    lane = lax.broadcasted_iota(jnp.int32, (8, LANES), 1)
    limits[...] = jnp.where(lane < RANK, lengths[0], lengths[1])
    bounds[...] = jnp.full((8, LANES), clip[0], F32)
    final = lax.axis_index("segment") == LAYERS - 1
    down = jnp.where(final, sent[...], kept[...]).T
    up_t = jnp.where(final, kept[...], sent[...]).T
    for i in range(STEPS):
        rows = pl.ds(i * STEP_ROWS, STEP_ROWS)
        copies[i][0].wait()
        first = jnp.concatenate([dot(act[e, rows], down, 1, 0) for e in range(2)], axis=1)
        copies[i][1].wait()
        last = jnp.concatenate([dot(cot[e, rows], up_t, 1, 0) for e in range(2)], axis=1)
        for j in range(STEP_ROWS // PIECE):
            part = slice(j * PIECE, (j + 1) * PIECE)
            out[i * (STEP_ROWS // PIECE) + j] = jnp.concatenate(
                [first[part], last[part]], axis=0
            ).astype(BF)


def project(lengths, clip, act, cot, sent, kept):
    return pl.pallas_call(
        project_body,
        in_specs=[SMEM, SMEM, HBM, HBM, VMEM, VMEM],
        out_specs=[VMEM] * 3,
        out_shape=[
            jax.ShapeDtypeStruct((CUTS, 2 * PIECE, LANES), BF),
            jax.ShapeDtypeStruct((8, LANES), jnp.int32),
            jax.ShapeDtypeStruct((8, LANES), F32),
        ],
        scratch_shapes=[
            pltpu.VMEM((2, SLOTS, WIDTH), BF),
            pltpu.VMEM((2, SLOTS, WIDTH), BF),
            pltpu.SemaphoreType.DMA((STEPS, 2)),
        ],
        compiler_params=pltpu.CompilerParams(vmem_limit_bytes=53 << 20),
        cost_estimate=pl.CostEstimate(flops=150000000, bytes_accessed=2800000, transcendentals=0),
    )(lengths, clip, act, cot, sent, kept)


def weave_body(partial, to_one, to_two, to_three, one, two, three, out):
    seg = lax.axis_index("segment")
    for k, own, other in ((1, to_three, one), (2, to_two, two), (3, to_one, three)):
        lower = seg >= k
        left = jnp.where(lower, other[HALF:], own[:HALF])
        right = jnp.where(lower, own[...], other[...])
        gram = dot(left, right, 1, 1)
        gram = jnp.concatenate([gram, jnp.zeros_like(gram)], axis=1)
        for q in range(4):
            tile = gram[q * 8 : (q + 1) * 8]
            out[(k - 1) * 4 + q, 2 * PIECE :] = jnp.concatenate(
                [tile, jnp.zeros_like(tile)], axis=0
            ).astype(BF)
    for t in range(CUTS):
        out[t, : 2 * PIECE] = partial[t]
    for t in range(12, CUTS):
        out[t, 2 * PIECE :] = jnp.zeros((EXTRA, LANES), BF)


def weave(partial, messages, peers):
    return pl.pallas_call(
        weave_body,
        in_specs=[VMEM] * 7,
        out_specs=VMEM,
        out_shape=jax.ShapeDtypeStruct((CUTS, 2 * PIECE + EXTRA, LANES), BF),
        compiler_params=pltpu.CompilerParams(vmem_limit_bytes=16 << 20),
        cost_estimate=pl.CostEstimate(flops=10000000, bytes_accessed=1000000, transcendentals=0),
    )(partial, *messages, *peers)


def reduce_body(limits, parts, out):
    base = lax.axis_index("tensor") * PIECE
    total = parts[0].astype(F32)
    for i in range(1, CUTS):
        total = total + parts[i].astype(F32)
    slot = lax.broadcasted_iota(jnp.int32, (PIECE, LANES), 0) + base
    live = slot < limits[:1]
    last = jnp.where(live, total[PIECE : 2 * PIECE], 0.0)
    message = jnp.concatenate([total[:PIECE], last, total[2 * PIECE :]], axis=0).astype(BF)
    for i in range(LAYERS * CUTS):
        out[i] = message


def reduce_parts(limits, parts):
    return pl.pallas_call(
        reduce_body,
        in_specs=[VMEM] * 2,
        out_specs=VMEM,
        out_shape=jax.ShapeDtypeStruct((LAYERS * CUTS, 2 * PIECE + EXTRA, LANES), BF),
        compiler_params=pltpu.CompilerParams(vmem_limit_bytes=16 << 20),
        cost_estimate=pl.CostEstimate(flops=200000, bytes_accessed=1300000, transcendentals=0),
    )(limits, parts)


def gradient_body(
    limits, gathered, one, two, three, act, cot,
    each, note,
    first, last, hidden, slopes, steep,
):
    seg = lax.axis_index("segment")
    packed = []
    for layer in range(LAYERS):
        tiles = []
        for t in range(CUTS):
            block = gathered[layer * CUTS + t].astype(F32)
            first[layer, t * PIECE : (t + 1) * PIECE] = block[:PIECE]
            last[layer, t * PIECE : (t + 1) * PIECE] = block[PIECE : 2 * PIECE]
            if t < 12:
                tiles.append(block[2 * PIECE : 2 * PIECE + 8, :RANK])
        packed.append(jnp.concatenate(tiles, axis=0))

    def gram_of(i, j):
        a, b = (i - j) % LAYERS - 1, (j - i) % LAYERS - 1
        gram = jnp.concatenate(
            [packed[i][a * HALF : (a + 1) * HALF], packed[j][b * HALF : (b + 1) * HALF]], axis=0
        )
        zero = jnp.zeros_like(gram)
        return jnp.concatenate(
            [jnp.concatenate([gram, zero], axis=1), jnp.concatenate([zero, gram], axis=1)], axis=0
        ).astype(BF)

    grams = {(i, j): gram_of(i, j) for j in range(LAYERS) for i in range(j)}

    for j in range(LAYERS):
        bottle = first[j]
        for i in range(j):
            bottle = bottle + dot(hidden[i], grams[i, j], 1, 0)
        value, slope = gelu_both(bottle)
        hidden[j] = value.astype(BF)
        steep[j] = slope
    for i in reversed(range(LAYERS)):
        spread = last[i]
        for j in range(i + 1, LAYERS):
            spread = spread + dot(slopes[j], grams[i, j], 1, 1)
        slopes[i] = (spread * steep[i]).astype(BF)

    slot = lax.broadcasted_iota(jnp.int32, (SLOTS, LANES), 0)
    live = slot < limits[:1]
    mine_h = jnp.where(live, hidden[seg].astype(F32), 0.0).T.astype(BF)
    mine_s = slopes[seg].astype(F32).T.astype(BF)

    lefts = []
    for k in range(1, LAYERS):
        peer = lax.rem(seg + LAYERS - k, LAYERS)
        lower = seg >= k
        left = jnp.where(lower, mine_s, mine_h)
        right = jnp.where(lower, hidden[peer], slopes[peer])
        mix = dot(left, right, 1, 0)
        mix = jnp.concatenate([mix[:RANK, :RANK], mix[RANK:, RANK:]], axis=0)
        lefts.append(
            jnp.concatenate([jnp.where(lower, mix, 0.0), jnp.where(lower, 0.0, mix)], axis=0)
        )
    left = jnp.concatenate(lefts, axis=1).astype(BF)
    peers = jnp.concatenate([one[...], two[...], three[...]], axis=0)
    each[...] = dot(left, peers, 1, 0)
    for e in range(2):
        rows = slice(e * RANK, (e + 1) * RANK)
        other = slice((2 + e) * RANK, (3 + e) * RANK)
        down_grad = each[rows] + dot(mine_s[rows], act[e], 1, 0)
        up_grad = each[other] + dot(mine_h[rows], cot[e], 1, 0)
        each[rows] = down_grad
        each[other] = up_grad
        square = jnp.sum(down_grad * down_grad + up_grad * up_grad)
        note[:, rows] = jnp.full((2 * CUTS, RANK), square, F32)


def gradients(limits, gathered, peers, act, cot):
    wide = (LAYERS, SLOTS, LANES)
    return pl.pallas_call(
        gradient_body,
        in_specs=[VMEM] * 7,
        out_specs=[VMEM] * 2,
        out_shape=[
            jax.ShapeDtypeStruct((4 * RANK, WIDTH), F32),
            jax.ShapeDtypeStruct((2 * CUTS, LANES), F32),
        ],
        scratch_shapes=[
            pltpu.VMEM(wide, F32),
            pltpu.VMEM(wide, F32),
            pltpu.VMEM(wide, BF),
            pltpu.VMEM(wide, BF),
            pltpu.VMEM(wide, F32),
        ],
        compiler_params=pltpu.CompilerParams(vmem_limit_bytes=32 << 20),
        cost_estimate=pl.CostEstimate(
            flops=600000000, bytes_accessed=5000000, transcendentals=200000
        ),
    )(limits, gathered, *peers, act, cot)


def share_body(each, theirs):
    give = pl.multiple_of((1 - lax.axis_index("dp")) * LOCAL, 128)
    theirs[...] = each[:, pl.ds(give, LOCAL)].astype(BF)


def share(each):
    return pl.pallas_call(
        share_body,
        in_specs=[VMEM],
        out_specs=VMEM,
        out_shape=jax.ShapeDtypeStruct((4 * RANK, LOCAL), BF),
        compiler_params=pltpu.CompilerParams(vmem_limit_bytes=16 << 20),
        cost_estimate=pl.CostEstimate(flops=100000, bytes_accessed=1000000, transcendentals=0),
    )(each)


def scale_body(bounds, notes, each, swapped, out_down, out_up):
    core = lax.axis_index("dp")
    ours = each.at[:, pl.ds(pl.multiple_of(core * LOCAL, 128), LOCAL)]
    row = lax.broadcasted_iota(jnp.int32, (2 * CUTS, LANES), 0)
    is_own = lax.rem(row, 2) == core
    values = notes[...]

    def factors(picked):
        total = jnp.sum(jnp.where(picked, values, 0.0), axis=0, keepdims=True)
        return bounds[:1] / (jnp.sqrt(total) + 0.01)

    own = factors(is_own)
    other = factors(jnp.logical_not(is_own))

    def combined(start):
        total = None
        for e in range(2):
            rows = slice(start + e * RANK, start + (e + 1) * RANK)
            at = slice(e * RANK, e * RANK + 1)
            term = own[:, at] * ours[rows] + other[:, at] * swapped[rows].astype(F32)
            total = term if total is None else total + term
        return total

    out_down[0] = combined(0)
    out_up[0] = combined(2 * RANK)


def scaled(bounds, notes, each, swapped):
    return pl.pallas_call(
        scale_body,
        in_specs=[VMEM] * 4,
        out_specs=[VMEM] * 2,
        out_shape=[
            jax.ShapeDtypeStruct((1, RANK, LOCAL), F32),
            jax.ShapeDtypeStruct((1, RANK, LOCAL), F32),
        ],
        compiler_params=pltpu.CompilerParams(vmem_limit_bytes=16 << 20),
        cost_estimate=pl.CostEstimate(flops=300000, bytes_accessed=900000, transcendentals=0),
    )(bounds, notes, each, swapped)


def shards(act_input, cotangent, lengths, clip_scale, adapt_down, adapt_up):
    seg = lax.axis_index("segment")
    up = adapt_up[0]
    down_t = adapt_down[0].T
    messages = [jnp.where(seg + k < LAYERS, up, down_t) for k in range(1, LAYERS)]
    peers = [
        lax.ppermute(messages[k - 1], "segment", [(i, (i + k) % LAYERS) for i in range(LAYERS)])
        for k in range(1, LAYERS)
    ]
    partial, limits, bounds = project(
        lengths, clip_scale, act_input, cotangent, messages[0], jnp.where(seg + 1 < LAYERS, down_t, up)
    )
    woven = weave(partial, messages, peers)
    parts = lax.all_to_all(woven, "tensor", 0, 0, tiled=True)
    message = reduce_parts(limits, parts)
    gathered = lax.all_to_all(message, ("segment", "tensor"), 0, 0, tiled=True)
    each, note = gradients(limits, gathered, peers, act_input, cotangent)
    swapped = lax.ppermute(share(each), "dp", [(0, 1), (1, 0)])
    notes = lax.all_to_all(note, ("tensor", "dp"), 0, 0, tiled=True)
    grad_down, grad_up = scaled(bounds, notes, each, swapped)
    return jnp.swapaxes(grad_down, 1, 2), grad_up


def solution(mesh):
    return jax.shard_map(
        shards,
        mesh=mesh,
        in_specs=(
            P("dp", None, "tensor"),
            P("dp", None, "tensor"),
            P("dp"),
            P("segment"),
            P("segment", "tensor", None),
            P("segment", None, "tensor"),
        ),
        out_specs=(P("segment", ("tensor", "dp"), None), P("segment", None, ("tensor", "dp"))),
        check_vma=False,
    )
```

```python
import jax
import jax.numpy as jnp
from jax import lax
from jax.experimental import pallas as pl
from jax.experimental.pallas import tpu as pltpu
from jax.sharding import PartitionSpec as P

SLOPE_C = 0.7978845608
CUBIC = 0.044715
BF = jnp.bfloat16
F32 = jnp.float32
VMEM = pl.BlockSpec(memory_space=pltpu.VMEM)
SMEM = pl.BlockSpec(memory_space=pltpu.SMEM)
HBM = pl.BlockSpec(memory_space=pltpu.HBM)

LAYERS = 4
CUTS = 16
SLOTS = 384
WIDTH = 768
RANK = 64
HALF = RANK // 2
LANES = 2 * RANK
PIECE = SLOTS // CUTS
EXTRA = 8
LOCAL = WIDTH // 2


def dot(a, b, ca, cb):
    return lax.dot_general(a, b, (((ca,), (cb,)), ((), ())), preferred_element_type=F32)


def gelu_both(values):
    squared = values * values
    tangent = jnp.tanh(values * (SLOPE_C + SLOPE_C * CUBIC * squared))
    half = 0.5 + 0.5 * tangent
    slope = half + values * (0.5 - 0.5 * tangent * tangent) * (
        SLOPE_C + 3.0 * SLOPE_C * CUBIC * squared
    )
    return values * half, slope


STEPS = 2
STEP_ROWS = SLOTS // STEPS


def project_body(
    lengths, clip, act_hbm, cot_hbm, sent, kept, out, limits, bounds, act, cot, sems
):
    copies = []
    for i in range(STEPS):
        rows = pl.ds(i * STEP_ROWS, STEP_ROWS)
        pair = []
        for j, (source, target) in enumerate(((act_hbm, act), (cot_hbm, cot))):
            copy = pltpu.make_async_copy(source.at[:, rows], target.at[:, rows], sems.at[i, j])
            copy.start()
            pair.append(copy)
        copies.append(pair)
    lane = lax.broadcasted_iota(jnp.int32, (8, LANES), 1)
    limits[...] = jnp.where(lane < RANK, lengths[0], lengths[1])
    bounds[...] = jnp.full((8, LANES), clip[0], F32)
    final = lax.axis_index("segment") == LAYERS - 1
    down = jnp.where(final, sent[...], kept[...]).T
    up_t = jnp.where(final, kept[...], sent[...]).T
    for i in range(STEPS):
        rows = pl.ds(i * STEP_ROWS, STEP_ROWS)
        copies[i][0].wait()
        first = jnp.concatenate([dot(act[e, rows], down, 1, 0) for e in range(2)], axis=1)
        copies[i][1].wait()
        last = jnp.concatenate([dot(cot[e, rows], up_t, 1, 0) for e in range(2)], axis=1)
        for j in range(STEP_ROWS // PIECE):
            part = slice(j * PIECE, (j + 1) * PIECE)
            out[i * (STEP_ROWS // PIECE) + j] = jnp.concatenate(
                [first[part], last[part]], axis=0
            ).astype(BF)


def project(lengths, clip, act, cot, sent, kept):
    return pl.pallas_call(
        project_body,
        in_specs=[SMEM, SMEM, HBM, HBM, VMEM, VMEM],
        out_specs=[VMEM] * 3,
        out_shape=[
            jax.ShapeDtypeStruct((CUTS, 2 * PIECE, LANES), BF),
            jax.ShapeDtypeStruct((8, LANES), jnp.int32),
            jax.ShapeDtypeStruct((8, LANES), F32),
        ],
        scratch_shapes=[
            pltpu.VMEM((2, SLOTS, WIDTH), BF),
            pltpu.VMEM((2, SLOTS, WIDTH), BF),
            pltpu.SemaphoreType.DMA((STEPS, 2)),
        ],
        compiler_params=pltpu.CompilerParams(vmem_limit_bytes=53 << 20),
        cost_estimate=pl.CostEstimate(flops=150000000, bytes_accessed=2800000, transcendentals=0),
    )(lengths, clip, act, cot, sent, kept)


def weave_body(partial, to_one, to_two, to_three, one, two, three, out):
    seg = lax.axis_index("segment")
    for k, own, other in ((1, to_three, one), (2, to_two, two), (3, to_one, three)):
        lower = seg >= k
        left = jnp.where(lower, other[HALF:], own[:HALF])
        right = jnp.where(lower, own[...], other[...])
        gram = dot(left, right, 1, 1)
        gram = jnp.concatenate([gram, jnp.zeros_like(gram)], axis=1)
        for q in range(4):
            t = (k - 1) * 4 + q
            tile = gram[q * 8 : (q + 1) * 8]
            out[t] = jnp.concatenate([partial[t].astype(F32), tile], axis=0).astype(BF)
    for t in range(12, CUTS):
        out[t] = jnp.concatenate(
            [partial[t].astype(F32), jnp.zeros((EXTRA, LANES), F32)], axis=0
        ).astype(BF)


def weave(partial, messages, peers):
    return pl.pallas_call(
        weave_body,
        in_specs=[VMEM] * 7,
        out_specs=VMEM,
        out_shape=jax.ShapeDtypeStruct((CUTS, 2 * PIECE + EXTRA, LANES), BF),
        compiler_params=pltpu.CompilerParams(vmem_limit_bytes=16 << 20),
        cost_estimate=pl.CostEstimate(flops=10000000, bytes_accessed=1000000, transcendentals=0),
    )(partial, *messages, *peers)


def reduce_body(limits, parts, out):
    base = lax.axis_index("tensor") * PIECE
    total = parts[0].astype(F32)
    for i in range(1, CUTS):
        total = total + parts[i].astype(F32)
    slot = lax.broadcasted_iota(jnp.int32, (PIECE, LANES), 0) + base
    live = slot < limits[:1]
    last = jnp.where(live, total[PIECE : 2 * PIECE], 0.0)
    message = jnp.concatenate([total[:PIECE], last, total[2 * PIECE :]], axis=0).astype(BF)
    for i in range(LAYERS * CUTS):
        out[i] = message


def reduce_parts(limits, parts):
    return pl.pallas_call(
        reduce_body,
        in_specs=[VMEM] * 2,
        out_specs=VMEM,
        out_shape=jax.ShapeDtypeStruct((LAYERS * CUTS, 2 * PIECE + EXTRA, LANES), BF),
        compiler_params=pltpu.CompilerParams(vmem_limit_bytes=16 << 20),
        cost_estimate=pl.CostEstimate(flops=200000, bytes_accessed=1300000, transcendentals=0),
    )(limits, parts)


def gradient_body(
    limits, gathered, one, two, three, act, cot,
    each, note,
    first, last, hidden, slopes, steep,
):
    seg = lax.axis_index("segment")
    packed = []
    for layer in range(LAYERS):
        tiles = []
        for t in range(CUTS):
            block = gathered[layer * CUTS + t].astype(F32)
            first[layer, t * PIECE : (t + 1) * PIECE] = block[:PIECE]
            last[layer, t * PIECE : (t + 1) * PIECE] = block[PIECE : 2 * PIECE]
            if t < 12:
                tiles.append(block[2 * PIECE : 2 * PIECE + 8, :RANK])
        packed.append(jnp.concatenate(tiles, axis=0))

    def gram_of(i, j):
        a, b = (i - j) % LAYERS - 1, (j - i) % LAYERS - 1
        gram = jnp.concatenate(
            [packed[i][a * HALF : (a + 1) * HALF], packed[j][b * HALF : (b + 1) * HALF]], axis=0
        )
        zero = jnp.zeros_like(gram)
        return jnp.concatenate(
            [jnp.concatenate([gram, zero], axis=1), jnp.concatenate([zero, gram], axis=1)], axis=0
        ).astype(BF)

    grams = {(i, j): gram_of(i, j) for j in range(LAYERS) for i in range(j)}

    for j in range(LAYERS):
        bottle = first[j]
        for i in range(j):
            bottle = bottle + dot(hidden[i], grams[i, j], 1, 0)
        value, slope = gelu_both(bottle)
        hidden[j] = value.astype(BF)
        steep[j] = slope
    for i in reversed(range(LAYERS)):
        spread = last[i]
        for j in range(i + 1, LAYERS):
            spread = spread + dot(slopes[j], grams[i, j], 1, 1)
        slopes[i] = (spread * steep[i]).astype(BF)

    slot = lax.broadcasted_iota(jnp.int32, (SLOTS, LANES), 0)
    live = slot < limits[:1]
    mine_h = jnp.where(live, hidden[seg].astype(F32), 0.0).T.astype(BF)
    mine_s = slopes[seg].astype(F32).T.astype(BF)

    lefts = []
    for k in range(1, LAYERS):
        peer = lax.rem(seg + LAYERS - k, LAYERS)
        lower = seg >= k
        left = jnp.where(lower, mine_s, mine_h)
        right = jnp.where(lower, hidden[peer], slopes[peer])
        mix = dot(left, right, 1, 0)
        mix = jnp.concatenate([mix[:RANK, :RANK], mix[RANK:, RANK:]], axis=0)
        lefts.append(
            jnp.concatenate([jnp.where(lower, mix, 0.0), jnp.where(lower, 0.0, mix)], axis=0)
        )
    left = jnp.concatenate(lefts, axis=1).astype(BF)
    peers = jnp.concatenate([one[...], two[...], three[...]], axis=0)
    each[...] = dot(left, peers, 1, 0)
    for e in range(2):
        rows = slice(e * RANK, (e + 1) * RANK)
        other = slice((2 + e) * RANK, (3 + e) * RANK)
        down_grad = each[rows] + dot(mine_s[rows], act[e], 1, 0)
        up_grad = each[other] + dot(mine_h[rows], cot[e], 1, 0)
        each[rows] = down_grad
        each[other] = up_grad
        square = jnp.sum(down_grad * down_grad + up_grad * up_grad)
        note[:, rows] = jnp.full((2 * CUTS, RANK), square, F32)


def gradients(limits, gathered, peers, act, cot):
    wide = (LAYERS, SLOTS, LANES)
    return pl.pallas_call(
        gradient_body,
        in_specs=[VMEM] * 7,
        out_specs=[VMEM] * 2,
        out_shape=[
            jax.ShapeDtypeStruct((4 * RANK, WIDTH), F32),
            jax.ShapeDtypeStruct((2 * CUTS, LANES), F32),
        ],
        scratch_shapes=[
            pltpu.VMEM(wide, F32),
            pltpu.VMEM(wide, F32),
            pltpu.VMEM(wide, BF),
            pltpu.VMEM(wide, BF),
            pltpu.VMEM(wide, F32),
        ],
        compiler_params=pltpu.CompilerParams(vmem_limit_bytes=32 << 20),
        cost_estimate=pl.CostEstimate(
            flops=600000000, bytes_accessed=5000000, transcendentals=200000
        ),
    )(limits, gathered, *peers, act, cot)


def share_body(each, theirs):
    give = pl.multiple_of((1 - lax.axis_index("dp")) * LOCAL, 128)
    theirs[...] = each[:, pl.ds(give, LOCAL)].astype(BF)


def share(each):
    return pl.pallas_call(
        share_body,
        in_specs=[VMEM],
        out_specs=VMEM,
        out_shape=jax.ShapeDtypeStruct((4 * RANK, LOCAL), BF),
        compiler_params=pltpu.CompilerParams(vmem_limit_bytes=16 << 20),
        cost_estimate=pl.CostEstimate(flops=100000, bytes_accessed=1000000, transcendentals=0),
    )(each)


def scale_body(bounds, notes, each, swapped, out_down, out_up):
    core = lax.axis_index("dp")
    ours = each.at[:, pl.ds(pl.multiple_of(core * LOCAL, 128), LOCAL)]
    row = lax.broadcasted_iota(jnp.int32, (2 * CUTS, LANES), 0)
    is_own = lax.rem(row, 2) == core
    values = notes[...]

    def factors(picked):
        total = jnp.sum(jnp.where(picked, values, 0.0), axis=0, keepdims=True)
        return bounds[:1] / (jnp.sqrt(total) + 0.01)

    own = factors(is_own)
    other = factors(jnp.logical_not(is_own))

    def combined(start):
        total = None
        for e in range(2):
            rows = slice(start + e * RANK, start + (e + 1) * RANK)
            at = slice(e * RANK, e * RANK + 1)
            term = own[:, at] * ours[rows] + other[:, at] * swapped[rows].astype(F32)
            total = term if total is None else total + term
        return total

    out_down[0] = combined(0)
    out_up[0] = combined(2 * RANK)


def scaled(bounds, notes, each, swapped):
    return pl.pallas_call(
        scale_body,
        in_specs=[VMEM] * 4,
        out_specs=[VMEM] * 2,
        out_shape=[
            jax.ShapeDtypeStruct((1, RANK, LOCAL), F32),
            jax.ShapeDtypeStruct((1, RANK, LOCAL), F32),
        ],
        compiler_params=pltpu.CompilerParams(vmem_limit_bytes=16 << 20),
        cost_estimate=pl.CostEstimate(flops=300000, bytes_accessed=900000, transcendentals=0),
    )(bounds, notes, each, swapped)


def shards(act_input, cotangent, lengths, clip_scale, adapt_down, adapt_up):
    seg = lax.axis_index("segment")
    up = adapt_up[0]
    down_t = adapt_down[0].T
    messages = [jnp.where(seg + k < LAYERS, up, down_t) for k in range(1, LAYERS)]
    peers = [
        lax.ppermute(messages[k - 1], "segment", [(i, (i + k) % LAYERS) for i in range(LAYERS)])
        for k in range(1, LAYERS)
    ]
    partial, limits, bounds = project(
        lengths, clip_scale, act_input, cotangent, messages[0], jnp.where(seg + 1 < LAYERS, down_t, up)
    )
    woven = weave(partial, messages, peers)
    parts = lax.all_to_all(woven, "tensor", 0, 0, tiled=True)
    message = reduce_parts(limits, parts)
    gathered = lax.all_to_all(message, ("segment", "tensor"), 0, 0, tiled=True)
    each, note = gradients(limits, gathered, peers, act_input, cotangent)
    swapped = lax.ppermute(share(each), "dp", [(0, 1), (1, 0)])
    notes = lax.all_to_all(note, ("tensor", "dp"), 0, 0, tiled=True)
    grad_down, grad_up = scaled(bounds, notes, each, swapped)
    return jnp.swapaxes(grad_down, 1, 2), grad_up


def solution(mesh):
    return jax.shard_map(
        shards,
        mesh=mesh,
        in_specs=(
            P("dp", None, "tensor"),
            P("dp", None, "tensor"),
            P("dp"),
            P("segment"),
            P("segment", "tensor", None),
            P("segment", None, "tensor"),
        ),
        out_specs=(P("segment", ("tensor", "dp"), None), P("segment", None, ("tensor", "dp"))),
        check_vma=False,
    )
```

```python
import jax
import jax.numpy as jnp
from jax import lax
from jax.experimental import pallas as pl
from jax.experimental.pallas import tpu as pltpu
from jax.sharding import PartitionSpec as P

SLOPE_C = 0.7978845608
CUBIC = 0.044715
BF = jnp.bfloat16
F32 = jnp.float32
VMEM = pl.BlockSpec(memory_space=pltpu.VMEM)
HBM = pl.BlockSpec(memory_space=pltpu.HBM)

LAYERS = 4
CUTS = 16
SLOTS = 384
WIDTH = 768
RANK = 64
HALF = RANK // 2
LANES = 2 * RANK
PIECE = SLOTS // CUTS
EXTRA = 8
LOCAL = WIDTH // 2


def dot(a, b, ca, cb):
    return lax.dot_general(a, b, (((ca,), (cb,)), ((), ())), preferred_element_type=F32)


def gelu_both(values):
    squared = values * values
    tangent = jnp.tanh(values * (SLOPE_C + SLOPE_C * CUBIC * squared))
    half = 0.5 + 0.5 * tangent
    slope = half + values * (0.5 - 0.5 * tangent * tangent) * (
        SLOPE_C + 3.0 * SLOPE_C * CUBIC * squared
    )
    return values * half, slope


STEPS = 2
STEP_ROWS = SLOTS // STEPS


def project_body(act_hbm, cot_hbm, sent, kept, out, act, cot, sems):
    copies = []
    for i in range(STEPS):
        rows = pl.ds(i * STEP_ROWS, STEP_ROWS)
        pair = []
        for j, (source, target) in enumerate(((act_hbm, act), (cot_hbm, cot))):
            copy = pltpu.make_async_copy(source.at[:, rows], target.at[:, rows], sems.at[i, j])
            copy.start()
            pair.append(copy)
        copies.append(pair)
    begin = lax.axis_index("segment") == 0
    down = jnp.where(begin, kept[...], sent[...]).T
    up_t = jnp.where(begin, sent[...], kept[...]).T
    for i in range(STEPS):
        rows = pl.ds(i * STEP_ROWS, STEP_ROWS)
        copies[i][0].wait()
        first = jnp.concatenate([dot(act[e, rows], down, 1, 0) for e in range(2)], axis=1)
        copies[i][1].wait()
        last = jnp.concatenate([dot(cot[e, rows], up_t, 1, 0) for e in range(2)], axis=1)
        for j in range(STEP_ROWS // PIECE):
            part = slice(j * PIECE, (j + 1) * PIECE)
            out[i * (STEP_ROWS // PIECE) + j] = jnp.concatenate(
                [first[part], last[part]], axis=0
            ).astype(BF)


def project(act, cot, sent, kept):
    return pl.pallas_call(
        project_body,
        in_specs=[HBM, HBM, VMEM, VMEM],
        out_specs=VMEM,
        out_shape=jax.ShapeDtypeStruct((CUTS, 2 * PIECE, LANES), BF),
        scratch_shapes=[
            pltpu.VMEM((2, SLOTS, WIDTH), BF),
            pltpu.VMEM((2, SLOTS, WIDTH), BF),
            pltpu.SemaphoreType.DMA((STEPS, 2)),
        ],
        compiler_params=pltpu.CompilerParams(vmem_limit_bytes=53 << 20),
        cost_estimate=pl.CostEstimate(flops=150000000, bytes_accessed=2800000, transcendentals=0),
    )(act, cot, sent, kept)


def weave_body(
    lengths, clip, partial, to_three, to_two, to_one, three, two, one, out, limits, bounds
):
    lane = lax.broadcasted_iota(jnp.int32, (8, LANES), 1)
    limits[...] = jnp.where(lane < RANK, lengths[:, :1], lengths[:, 1:])
    bounds[...] = jnp.broadcast_to(clip[...], (8, LANES))
    seg = lax.axis_index("segment")
    for k, own, other in ((1, to_three, one), (2, to_two, two), (3, to_one, three)):
        lower = seg >= k
        left = jnp.where(lower, other[HALF:], own[:HALF])
        right = jnp.where(lower, own[...], other[...])
        gram = dot(left, right, 1, 1)
        gram = jnp.concatenate([gram, jnp.zeros_like(gram)], axis=1)
        for q in range(4):
            t = (k - 1) * 4 + q
            tile = gram[q * 8 : (q + 1) * 8]
            out[t] = jnp.concatenate([partial[t].astype(F32), tile], axis=0).astype(BF)
    for t in range(12, CUTS):
        out[t] = jnp.concatenate(
            [partial[t].astype(F32), jnp.zeros((EXTRA, LANES), F32)], axis=0
        ).astype(BF)


def weave(lengths, clip, partial, messages, peers):
    return pl.pallas_call(
        weave_body,
        in_specs=[VMEM] * 9,
        out_specs=[VMEM] * 3,
        out_shape=[
            jax.ShapeDtypeStruct((CUTS, 2 * PIECE + EXTRA, LANES), BF),
            jax.ShapeDtypeStruct((8, LANES), jnp.int32),
            jax.ShapeDtypeStruct((8, LANES), F32),
        ],
        compiler_params=pltpu.CompilerParams(vmem_limit_bytes=16 << 20),
        cost_estimate=pl.CostEstimate(flops=10000000, bytes_accessed=1000000, transcendentals=0),
    )(lengths, clip, partial, messages[2], messages[1], messages[0], peers[2], peers[1], peers[0])


def reduce_body(limits, parts, out):
    base = lax.axis_index("tensor") * PIECE
    total = parts[0].astype(F32)
    for i in range(1, CUTS):
        total = total + parts[i].astype(F32)
    slot = lax.broadcasted_iota(jnp.int32, (PIECE, LANES), 0) + base
    live = slot < limits[:1]
    last = jnp.where(live, total[PIECE : 2 * PIECE], 0.0)
    message = jnp.concatenate([total[:PIECE], last, total[2 * PIECE :]], axis=0).astype(BF)
    for i in range(LAYERS * CUTS):
        out[i] = message


def reduce_parts(limits, parts):
    return pl.pallas_call(
        reduce_body,
        in_specs=[VMEM] * 2,
        out_specs=VMEM,
        out_shape=jax.ShapeDtypeStruct((LAYERS * CUTS, 2 * PIECE + EXTRA, LANES), BF),
        compiler_params=pltpu.CompilerParams(vmem_limit_bytes=16 << 20),
        cost_estimate=pl.CostEstimate(flops=200000, bytes_accessed=1300000, transcendentals=0),
    )(limits, parts)


def gradient_body(
    limits, gathered, one, two, three, act, cot,
    each, note,
    first, last, hidden, slopes, steep,
):
    seg = lax.axis_index("segment")
    packed = []
    for layer in range(LAYERS):
        tiles = []
        for t in range(CUTS):
            block = gathered[layer * CUTS + t].astype(F32)
            first[layer, t * PIECE : (t + 1) * PIECE] = block[:PIECE]
            last[layer, t * PIECE : (t + 1) * PIECE] = block[PIECE : 2 * PIECE]
            if t < 12:
                tiles.append(block[2 * PIECE : 2 * PIECE + 8, :RANK])
        packed.append(jnp.concatenate(tiles, axis=0))

    def gram_of(i, j):
        a, b = (i - j) % LAYERS - 1, (j - i) % LAYERS - 1
        gram = jnp.concatenate(
            [packed[i][a * HALF : (a + 1) * HALF], packed[j][b * HALF : (b + 1) * HALF]], axis=0
        )
        zero = jnp.zeros_like(gram)
        return jnp.concatenate(
            [jnp.concatenate([gram, zero], axis=1), jnp.concatenate([zero, gram], axis=1)], axis=0
        ).astype(BF)

    grams = {(i, j): gram_of(i, j) for j in range(LAYERS) for i in range(j)}

    for j in range(LAYERS):
        bottle = first[j]
        for i in range(j):
            bottle = bottle + dot(hidden[i], grams[i, j], 1, 0)
        value, slope = gelu_both(bottle)
        hidden[j] = value.astype(BF)
        steep[j] = slope
    for i in reversed(range(LAYERS)):
        spread = last[i]
        for j in range(i + 1, LAYERS):
            spread = spread + dot(slopes[j], grams[i, j], 1, 1)
        slopes[i] = (spread * steep[i]).astype(BF)

    slot = lax.broadcasted_iota(jnp.int32, (SLOTS, LANES), 0)
    live = slot < limits[:1]
    mine_h = jnp.where(live, hidden[seg].astype(F32), 0.0).T.astype(BF)
    mine_s = slopes[seg].astype(F32).T.astype(BF)

    lefts = []
    for k in range(1, LAYERS):
        peer = lax.rem(seg + LAYERS - k, LAYERS)
        lower = seg >= k
        left = jnp.where(lower, mine_s, mine_h)
        right = jnp.where(lower, hidden[peer], slopes[peer])
        mix = dot(left, right, 1, 0)
        mix = jnp.concatenate([mix[:RANK, :RANK], mix[RANK:, RANK:]], axis=0)
        lefts.append(
            jnp.concatenate([jnp.where(lower, mix, 0.0), jnp.where(lower, 0.0, mix)], axis=0)
        )
    left = jnp.concatenate(lefts, axis=1).astype(BF)
    peers = jnp.concatenate([one[...], two[...], three[...]], axis=0)
    each[...] = dot(left, peers, 1, 0)
    for e in range(2):
        rows = slice(e * RANK, (e + 1) * RANK)
        other = slice((2 + e) * RANK, (3 + e) * RANK)
        down_grad = each[rows] + dot(mine_s[rows], act[e], 1, 0)
        up_grad = each[other] + dot(mine_h[rows], cot[e], 1, 0)
        each[rows] = down_grad
        each[other] = up_grad
        square = jnp.sum(down_grad * down_grad + up_grad * up_grad)
        note[:, rows] = jnp.full((2 * CUTS, RANK), square, F32)


def gradients(limits, gathered, peers, act, cot):
    wide = (LAYERS, SLOTS, LANES)
    return pl.pallas_call(
        gradient_body,
        in_specs=[VMEM] * 7,
        out_specs=[VMEM] * 2,
        out_shape=[
            jax.ShapeDtypeStruct((4 * RANK, WIDTH), F32),
            jax.ShapeDtypeStruct((2 * CUTS, LANES), F32),
        ],
        scratch_shapes=[
            pltpu.VMEM(wide, F32),
            pltpu.VMEM(wide, F32),
            pltpu.VMEM(wide, BF),
            pltpu.VMEM(wide, BF),
            pltpu.VMEM(wide, F32),
        ],
        compiler_params=pltpu.CompilerParams(vmem_limit_bytes=32 << 20),
        cost_estimate=pl.CostEstimate(
            flops=600000000, bytes_accessed=5000000, transcendentals=200000
        ),
    )(limits, gathered, peers[0], peers[1], peers[2], act, cot)


def share_body(each, theirs):
    give = pl.multiple_of((1 - lax.axis_index("dp")) * LOCAL, 128)
    theirs[...] = each[:, pl.ds(give, LOCAL)].astype(BF)


def share(each):
    return pl.pallas_call(
        share_body,
        in_specs=[VMEM],
        out_specs=VMEM,
        out_shape=jax.ShapeDtypeStruct((4 * RANK, LOCAL), BF),
        compiler_params=pltpu.CompilerParams(vmem_limit_bytes=16 << 20),
        cost_estimate=pl.CostEstimate(flops=100000, bytes_accessed=1000000, transcendentals=0),
    )(each)


def scale_body(bounds, notes, each, swapped, out_down, out_up):
    core = lax.axis_index("dp")
    ours = each.at[:, pl.ds(pl.multiple_of(core * LOCAL, 128), LOCAL)]
    row = lax.broadcasted_iota(jnp.int32, (2 * CUTS, LANES), 0)
    is_own = lax.rem(row, 2) == core
    values = notes[...]

    def factors(picked):
        total = jnp.sum(jnp.where(picked, values, 0.0), axis=0, keepdims=True)
        return bounds[:1] / (jnp.sqrt(total) + 0.01)

    own = factors(is_own)
    other = factors(jnp.logical_not(is_own))

    def combined(start):
        total = None
        for e in range(2):
            rows = slice(start + e * RANK, start + (e + 1) * RANK)
            at = slice(e * RANK, e * RANK + 1)
            term = own[:, at] * ours[rows] + other[:, at] * swapped[rows].astype(F32)
            total = term if total is None else total + term
        return total

    out_down[0] = combined(0)
    out_up[0] = combined(2 * RANK)


def scaled(bounds, notes, each, swapped):
    return pl.pallas_call(
        scale_body,
        in_specs=[VMEM] * 4,
        out_specs=[VMEM] * 2,
        out_shape=[
            jax.ShapeDtypeStruct((1, RANK, LOCAL), F32),
            jax.ShapeDtypeStruct((1, RANK, LOCAL), F32),
        ],
        compiler_params=pltpu.CompilerParams(vmem_limit_bytes=16 << 20),
        cost_estimate=pl.CostEstimate(flops=300000, bytes_accessed=900000, transcendentals=0),
    )(bounds, notes, each, swapped)


def shards(act_input, cotangent, lengths, clip_scale, adapt_down, adapt_up):
    seg = lax.axis_index("segment")
    up = adapt_up[0]
    down_t = adapt_down[0].T
    messages = [jnp.where(seg + k < LAYERS, up, down_t) for k in range(1, LAYERS)]
    peers = [
        lax.ppermute(messages[k - 1], "segment", [(i, (i + k) % LAYERS) for i in range(LAYERS)])
        for k in range(1, LAYERS)
    ]
    partial = project(
        act_input, cotangent, messages[2], jnp.where(seg + 3 < LAYERS, down_t, up)
    )
    woven, limits, bounds = weave(
        lengths.reshape(1, 2), clip_scale.reshape(1, 1), partial, messages, peers
    )
    parts = lax.all_to_all(woven, "tensor", 0, 0, tiled=True)
    message = reduce_parts(limits, parts)
    gathered = lax.all_to_all(message, ("segment", "tensor"), 0, 0, tiled=True)
    each, note = gradients(limits, gathered, peers, act_input, cotangent)
    swapped = lax.ppermute(share(each), "dp", [(0, 1), (1, 0)])
    notes = lax.all_to_all(note, ("tensor", "dp"), 0, 0, tiled=True)
    grad_down, grad_up = scaled(bounds, notes, each, swapped)
    return jnp.swapaxes(grad_down, 1, 2), grad_up


def solution(mesh):
    return jax.shard_map(
        shards,
        mesh=mesh,
        in_specs=(
            P("dp", None, "tensor"),
            P("dp", None, "tensor"),
            P("dp"),
            P("segment"),
            P("segment", "tensor", None),
            P("segment", None, "tensor"),
        ),
        out_specs=(P("segment", ("tensor", "dp"), None), P("segment", None, ("tensor", "dp"))),
        check_vma=False,
    )
```

```python
import jax
import jax.numpy as jnp
from jax import lax
from jax.experimental import pallas as pl
from jax.experimental.pallas import tpu as pltpu
from jax.sharding import PartitionSpec as P

SLOPE_C = 0.7978845608
CUBIC = 0.044715
BF = jnp.bfloat16
F32 = jnp.float32
VMEM = pl.BlockSpec(memory_space=pltpu.VMEM)
HBM = pl.BlockSpec(memory_space=pltpu.HBM)

LAYERS = 4
CUTS = 16
SLOTS = 384
WIDTH = 768
RANK = 64
HALF = RANK // 2
LANES = 2 * RANK
PIECE = SLOTS // CUTS
EXTRA = 8
LOCAL = WIDTH // 2


def dot(a, b, ca, cb):
    return lax.dot_general(a, b, (((ca,), (cb,)), ((), ())), preferred_element_type=F32)


def gelu_both(values):
    squared = values * values
    tangent = jnp.tanh(values * (SLOPE_C + SLOPE_C * CUBIC * squared))
    half = 0.5 + 0.5 * tangent
    slope = half + values * (0.5 - 0.5 * tangent * tangent) * (
        SLOPE_C + 3.0 * SLOPE_C * CUBIC * squared
    )
    return values * half, slope


STEPS = 1
STEP_ROWS = SLOTS // STEPS


def project_body(act_hbm, cot_hbm, sent, kept, out, act, cot, sems):
    copies = []
    for i in range(STEPS):
        rows = pl.ds(i * STEP_ROWS, STEP_ROWS)
        pair = []
        for j, (source, target) in enumerate(((act_hbm, act), (cot_hbm, cot))):
            copy = pltpu.make_async_copy(source.at[:, rows], target.at[:, rows], sems.at[i, j])
            copy.start()
            pair.append(copy)
        copies.append(pair)
    begin = lax.axis_index("segment") == 0
    down = jnp.where(begin, kept[...], sent[...]).T
    up_t = jnp.where(begin, sent[...], kept[...]).T
    for i in range(STEPS):
        rows = pl.ds(i * STEP_ROWS, STEP_ROWS)
        copies[i][0].wait()
        first = jnp.concatenate([dot(act[e, rows], down, 1, 0) for e in range(2)], axis=1)
        copies[i][1].wait()
        last = jnp.concatenate([dot(cot[e, rows], up_t, 1, 0) for e in range(2)], axis=1)
        for j in range(STEP_ROWS // PIECE):
            part = slice(j * PIECE, (j + 1) * PIECE)
            out[i * (STEP_ROWS // PIECE) + j] = jnp.concatenate(
                [first[part], last[part]], axis=0
            ).astype(BF)


def project(act, cot, sent, kept):
    return pl.pallas_call(
        project_body,
        in_specs=[HBM, HBM, VMEM, VMEM],
        out_specs=VMEM,
        out_shape=jax.ShapeDtypeStruct((CUTS, 2 * PIECE, LANES), BF),
        scratch_shapes=[
            pltpu.VMEM((2, SLOTS, WIDTH), BF),
            pltpu.VMEM((2, SLOTS, WIDTH), BF),
            pltpu.SemaphoreType.DMA((STEPS, 2)),
        ],
        compiler_params=pltpu.CompilerParams(vmem_limit_bytes=53 << 20),
        cost_estimate=pl.CostEstimate(flops=150000000, bytes_accessed=2800000, transcendentals=0),
    )(act, cot, sent, kept)


def weave_body(
    lengths, clip, partial, to_three, to_two, one, two, out, limits, bounds
):
    lane = lax.broadcasted_iota(jnp.int32, (8, LANES), 1)
    limits[...] = jnp.where(lane < RANK, lengths[:, :1], lengths[:, 1:])
    bounds[...] = jnp.broadcast_to(clip[...], (8, LANES))
    seg = lax.axis_index("segment")
    lower = seg >= 1
    left = jnp.where(lower, one[...], to_three[...])
    right = jnp.where(lower, to_three[...], one[...])
    near = dot(left, right, 1, 1)
    lower = seg >= 2
    left = jnp.where(lower, two[HALF:], to_two[:HALF])
    right = jnp.where(lower, to_two[...], two[...])
    gram = jnp.concatenate([near, dot(left, right, 1, 1)], axis=0)
    gram = jnp.concatenate([gram, jnp.zeros_like(gram)], axis=1)
    for t in range(12):
        tile = gram[t * 8 : (t + 1) * 8]
        out[t] = jnp.concatenate([partial[t].astype(F32), tile], axis=0).astype(BF)
    for t in range(12, CUTS):
        out[t] = jnp.concatenate(
            [partial[t].astype(F32), jnp.zeros((EXTRA, LANES), F32)], axis=0
        ).astype(BF)


def weave(lengths, clip, partial, messages, peers):
    return pl.pallas_call(
        weave_body,
        in_specs=[VMEM] * 7,
        out_specs=[VMEM] * 3,
        out_shape=[
            jax.ShapeDtypeStruct((CUTS, 2 * PIECE + EXTRA, LANES), BF),
            jax.ShapeDtypeStruct((8, LANES), jnp.int32),
            jax.ShapeDtypeStruct((8, LANES), F32),
        ],
        compiler_params=pltpu.CompilerParams(vmem_limit_bytes=16 << 20),
        cost_estimate=pl.CostEstimate(flops=10000000, bytes_accessed=1000000, transcendentals=0),
    )(lengths, clip, partial, messages[2], messages[1], peers[0], peers[1])


def reduce_body(limits, parts, far, out):
    base = lax.axis_index("tensor") * PIECE
    total = parts[0].astype(F32)
    for i in range(1, CUTS):
        total = total + parts[i].astype(F32)
    slot = lax.broadcasted_iota(jnp.int32, (PIECE, LANES), 0) + base
    live = slot < limits[:1]
    last = jnp.where(live, total[PIECE : 2 * PIECE], 0.0)
    message = jnp.concatenate([total[:PIECE], last, total[2 * PIECE :]], axis=0).astype(BF)
    for i in range(LAYERS * CUTS):
        out[i] = message


def reduce_parts(limits, parts, far):
    return pl.pallas_call(
        reduce_body,
        in_specs=[VMEM] * 3,
        out_specs=VMEM,
        out_shape=jax.ShapeDtypeStruct((LAYERS * CUTS, 2 * PIECE + EXTRA, LANES), BF),
        compiler_params=pltpu.CompilerParams(vmem_limit_bytes=16 << 20),
        cost_estimate=pl.CostEstimate(flops=200000, bytes_accessed=1300000, transcendentals=0),
    )(limits, parts, far)


def gradient_body(
    limits, gathered, one, two, three, act, cot,
    each, note, theirs,
    first, last, hidden, slopes, steep,
):
    seg = lax.axis_index("segment")
    packed = []
    for layer in range(LAYERS):
        tiles = []
        for t in range(CUTS):
            block = gathered[layer * CUTS + t].astype(F32)
            first[layer, t * PIECE : (t + 1) * PIECE] = block[:PIECE]
            last[layer, t * PIECE : (t + 1) * PIECE] = block[PIECE : 2 * PIECE]
            if t < 12:
                tiles.append(block[2 * PIECE : 2 * PIECE + 8, :RANK])
        packed.append(jnp.concatenate(tiles, axis=0))

    def gram_of(i, j):
        if j - i == 2:
            gram = jnp.concatenate([packed[i][RANK:], packed[j][RANK:]], axis=0)
        else:
            gram = packed[(i + 1 if j - i == 1 else 0)][:RANK]
        zero = jnp.zeros_like(gram)
        return jnp.concatenate(
            [jnp.concatenate([gram, zero], axis=1), jnp.concatenate([zero, gram], axis=1)], axis=0
        ).astype(BF)

    grams = {(i, j): gram_of(i, j) for j in range(LAYERS) for i in range(j)}

    for j in range(LAYERS):
        bottle = first[j]
        for i in range(j):
            bottle = bottle + dot(hidden[i], grams[i, j], 1, 0)
        value, slope = gelu_both(bottle)
        hidden[j] = value.astype(BF)
        steep[j] = slope
    for i in reversed(range(LAYERS)):
        spread = last[i]
        for j in range(i + 1, LAYERS):
            spread = spread + dot(slopes[j], grams[i, j], 1, 1)
        slopes[i] = (spread * steep[i]).astype(BF)

    slot = lax.broadcasted_iota(jnp.int32, (SLOTS, LANES), 0)
    live = slot < limits[:1]
    mine_h = jnp.where(live, hidden[seg].astype(F32), 0.0).T.astype(BF)
    mine_s = slopes[seg].astype(F32).T.astype(BF)

    lefts = []
    for k in range(1, LAYERS):
        peer = lax.rem(seg + LAYERS - k, LAYERS)
        lower = seg >= k
        left = jnp.where(lower, mine_s, mine_h)
        right = jnp.where(lower, hidden[peer], slopes[peer])
        mix = dot(left, right, 1, 0)
        mix = jnp.concatenate([mix[:RANK, :RANK], mix[RANK:, RANK:]], axis=0)
        lefts.append(
            jnp.concatenate([jnp.where(lower, mix, 0.0), jnp.where(lower, 0.0, mix)], axis=0)
        )
    left = jnp.concatenate(lefts, axis=1).astype(BF)
    peers = jnp.concatenate([one[...], two[...], three[...]], axis=0)
    extra = dot(left, peers, 1, 0)
    give = pl.multiple_of((1 - lax.axis_index("dp")) * LOCAL, 128)
    for e in range(2):
        rows = slice(e * RANK, (e + 1) * RANK)
        other = slice((2 + e) * RANK, (3 + e) * RANK)
        down_grad = extra[rows] + dot(mine_s[rows], act[e], 1, 0)
        up_grad = extra[other] + dot(mine_h[rows], cot[e], 1, 0)
        each[rows] = down_grad
        each[other] = up_grad
        square = jnp.sum(down_grad * down_grad + up_grad * up_grad)
        note[:, rows] = jnp.full((2 * CUTS, RANK), square, F32)
    theirs[...] = each[:, pl.ds(give, LOCAL)].astype(BF)


def gradients(limits, gathered, peers, act, cot):
    wide = (LAYERS, SLOTS, LANES)
    return pl.pallas_call(
        gradient_body,
        in_specs=[VMEM] * 7,
        out_specs=[VMEM] * 3,
        out_shape=[
            jax.ShapeDtypeStruct((4 * RANK, WIDTH), F32),
            jax.ShapeDtypeStruct((2 * CUTS, LANES), F32),
            jax.ShapeDtypeStruct((4 * RANK, LOCAL), BF),
        ],
        scratch_shapes=[
            pltpu.VMEM(wide, F32),
            pltpu.VMEM(wide, F32),
            pltpu.VMEM(wide, BF),
            pltpu.VMEM(wide, BF),
            pltpu.VMEM(wide, F32),
        ],
        compiler_params=pltpu.CompilerParams(vmem_limit_bytes=32 << 20),
        cost_estimate=pl.CostEstimate(
            flops=600000000, bytes_accessed=5000000, transcendentals=200000
        ),
    )(limits, gathered, peers[0], peers[1], peers[2], act, cot)


def scale_body(bounds, notes, each, swapped, out_down, out_up):
    core = lax.axis_index("dp")
    ours = each.at[:, pl.ds(pl.multiple_of(core * LOCAL, 128), LOCAL)]
    row = lax.broadcasted_iota(jnp.int32, (2 * CUTS, LANES), 0)
    is_own = lax.rem(row, 2) == core
    values = notes[...]

    def factors(picked):
        total = jnp.sum(jnp.where(picked, values, 0.0), axis=0, keepdims=True)
        return bounds[:1] / (jnp.sqrt(total) + 0.01)

    own = factors(is_own)
    other = factors(jnp.logical_not(is_own))

    def combined(start):
        total = None
        for e in range(2):
            rows = slice(start + e * RANK, start + (e + 1) * RANK)
            at = slice(e * RANK, e * RANK + 1)
            term = own[:, at] * ours[rows] + other[:, at] * swapped[rows].astype(F32)
            total = term if total is None else total + term
        return total

    out_down[0] = combined(0)
    out_up[0] = combined(2 * RANK)


def scaled(bounds, notes, each, swapped):
    return pl.pallas_call(
        scale_body,
        in_specs=[VMEM] * 4,
        out_specs=[VMEM] * 2,
        out_shape=[
            jax.ShapeDtypeStruct((1, RANK, LOCAL), F32),
            jax.ShapeDtypeStruct((1, RANK, LOCAL), F32),
        ],
        compiler_params=pltpu.CompilerParams(vmem_limit_bytes=16 << 20),
        cost_estimate=pl.CostEstimate(flops=300000, bytes_accessed=900000, transcendentals=0),
    )(bounds, notes, each, swapped)


def shards(act_input, cotangent, lengths, clip_scale, adapt_down, adapt_up):
    seg = lax.axis_index("segment")
    up = adapt_up[0]
    down_t = adapt_down[0].T
    messages = [jnp.where(seg + k < LAYERS, up, down_t) for k in range(1, LAYERS)]
    peers = [
        lax.ppermute(messages[k - 1], "segment", [(i, (i + k) % LAYERS) for i in range(LAYERS)])
        for k in range(1, LAYERS)
    ]
    partial = project(
        act_input, cotangent, messages[2], jnp.where(seg + 3 < LAYERS, down_t, up)
    )
    woven, limits, bounds = weave(
        lengths.reshape(1, 2), clip_scale.reshape(1, 1), partial, messages, peers
    )
    parts = lax.all_to_all(woven, "tensor", 0, 0, tiled=True)
    message = reduce_parts(limits, parts, peers[2])
    gathered = lax.all_to_all(message, ("segment", "tensor"), 0, 0, tiled=True)
    each, note, theirs = gradients(limits, gathered, peers, act_input, cotangent)
    swapped = lax.ppermute(theirs, "dp", [(0, 1), (1, 0)])
    notes = lax.all_to_all(note, ("tensor", "dp"), 0, 0, tiled=True)
    grad_down, grad_up = scaled(bounds, notes, each, swapped)
    return jnp.swapaxes(grad_down, 1, 2), grad_up


def solution(mesh):
    return jax.shard_map(
        shards,
        mesh=mesh,
        in_specs=(
            P("dp", None, "tensor"),
            P("dp", None, "tensor"),
            P("dp"),
            P("segment"),
            P("segment", "tensor", None),
            P("segment", None, "tensor"),
        ),
        out_specs=(P("segment", ("tensor", "dp"), None), P("segment", None, ("tensor", "dp"))),
        check_vma=False,
    )
```

```python
import jax
import jax.numpy as jnp
from jax import lax
from jax.experimental import pallas as pl
from jax.experimental.pallas import tpu as pltpu
from jax.sharding import PartitionSpec as P

SLOPE_C = 0.7978845608
CUBIC = 0.044715
BF = jnp.bfloat16
F32 = jnp.float32
VMEM = pl.BlockSpec(memory_space=pltpu.VMEM)
HBM = pl.BlockSpec(memory_space=pltpu.HBM)

LAYERS = 4
CUTS = 16
SLOTS = 384
WIDTH = 768
RANK = 64
HALF = RANK // 2
LANES = 2 * RANK
PIECE = SLOTS // CUTS
EXTRA = 8
LOCAL = WIDTH // 2


def dot(a, b, ca, cb):
    return lax.dot_general(a, b, (((ca,), (cb,)), ((), ())), preferred_element_type=F32)


def gelu_both(values):
    squared = values * values
    tangent = jnp.tanh(values * (SLOPE_C + SLOPE_C * CUBIC * squared))
    half = 0.5 + 0.5 * tangent
    slope = half + values * (0.5 - 0.5 * tangent * tangent) * (
        SLOPE_C + 3.0 * SLOPE_C * CUBIC * squared
    )
    return values * half, slope


STEPS = 1
STEP_ROWS = SLOTS // STEPS


def project_body(act_hbm, cot_hbm, sent, kept, out, act, cot, sems):
    copies = []
    for i in range(STEPS):
        rows = pl.ds(i * STEP_ROWS, STEP_ROWS)
        pair = []
        for j, (source, target) in enumerate(((act_hbm, act), (cot_hbm, cot))):
            copy = pltpu.make_async_copy(source.at[:, rows], target.at[:, rows], sems.at[i, j])
            copy.start()
            pair.append(copy)
        copies.append(pair)
    begin = lax.axis_index("segment") == 0
    down = jnp.where(begin, kept[...], sent[...]).T
    up_t = jnp.where(begin, sent[...], kept[...]).T
    for i in range(STEPS):
        rows = pl.ds(i * STEP_ROWS, STEP_ROWS)
        copies[i][0].wait()
        first = jnp.concatenate([dot(act[e, rows], down, 1, 0) for e in range(2)], axis=1)
        copies[i][1].wait()
        last = jnp.concatenate([dot(cot[e, rows], up_t, 1, 0) for e in range(2)], axis=1)
        for j in range(STEP_ROWS // PIECE):
            part = slice(j * PIECE, (j + 1) * PIECE)
            out[i * (STEP_ROWS // PIECE) + j] = jnp.concatenate(
                [first[part], last[part]], axis=0
            ).astype(BF)


def project(act, cot, sent, kept):
    return pl.pallas_call(
        project_body,
        in_specs=[HBM, HBM, VMEM, VMEM],
        out_specs=VMEM,
        out_shape=jax.ShapeDtypeStruct((CUTS, 2 * PIECE, LANES), BF),
        scratch_shapes=[
            pltpu.VMEM((2, SLOTS, WIDTH), BF),
            pltpu.VMEM((2, SLOTS, WIDTH), BF),
            pltpu.SemaphoreType.DMA((STEPS, 2)),
        ],
        compiler_params=pltpu.CompilerParams(vmem_limit_bytes=53 << 20),
        cost_estimate=pl.CostEstimate(flops=150000000, bytes_accessed=2800000, transcendentals=0),
    )(act, cot, sent, kept)


def weave_body(
    lengths, clip, partial, to_two, to_three, one, two, out, limits, bounds,
    woven, sems,
):
    lane = lax.broadcasted_iota(jnp.int32, (8, LANES), 1)
    limits[...] = jnp.where(lane < RANK, lengths[:, :1], lengths[:, 1:])
    bounds[...] = jnp.broadcast_to(clip[...], (8, LANES))
    seg = lax.axis_index("segment")
    lower = seg >= 1
    left = jnp.where(lower, one[...], to_three[...])
    right = jnp.where(lower, to_three[...], one[...])
    near = dot(left, right, 1, 1)
    lower = seg >= 2
    left = jnp.where(lower, two[HALF:], to_two[:HALF])
    right = jnp.where(lower, to_two[...], two[...])
    stores = []

    def store(first, last):
        block = pl.ds(first, last - first)
        copy = pltpu.make_async_copy(woven.at[block], out.at[block], sems.at[len(stores)])
        copy.start()
        stores.append(copy)

    def fill(first, tiles):
        for i in range(tiles.shape[0] // 8):
            tile = tiles[i * 8 : (i + 1) * 8]
            tile = jnp.concatenate([tile, jnp.zeros_like(tile)], axis=1)
            woven[first + i] = jnp.concatenate(
                [partial[first + i].astype(F32), tile], axis=0
            ).astype(BF)

    fill(12, jnp.zeros((32, RANK), F32))
    store(12, CUTS)
    fill(0, near)
    store(0, 8)
    fill(8, dot(left, right, 1, 1))
    store(8, 12)
    for copy in stores:
        copy.wait()


def weave(lengths, clip, partial, messages, peers):
    return pl.pallas_call(
        weave_body,
        in_specs=[VMEM] * 7,
        out_specs=[HBM] + [VMEM] * 2,
        out_shape=[
            jax.ShapeDtypeStruct((CUTS, 2 * PIECE + EXTRA, LANES), BF),
            jax.ShapeDtypeStruct((8, LANES), jnp.int32),
            jax.ShapeDtypeStruct((8, LANES), F32),
        ],
        scratch_shapes=[
            pltpu.VMEM((CUTS, 2 * PIECE + EXTRA, LANES), BF),
            pltpu.SemaphoreType.DMA((3,)),
        ],
        compiler_params=pltpu.CompilerParams(vmem_limit_bytes=16 << 20),
        cost_estimate=pl.CostEstimate(flops=10000000, bytes_accessed=1000000, transcendentals=0),
    )(lengths, clip, partial, messages[1], messages[2], peers[0], peers[1])


def reduce_body(limits, parts, far, out):
    base = lax.axis_index("tensor") * PIECE
    total = parts[0].astype(F32)
    for i in range(1, CUTS):
        total = total + parts[i].astype(F32)
    slot = lax.broadcasted_iota(jnp.int32, (PIECE, LANES), 0) + base
    live = slot < limits[:1]
    last = jnp.where(live, total[PIECE : 2 * PIECE], 0.0)
    message = jnp.concatenate([total[:PIECE], last, total[2 * PIECE :]], axis=0).astype(BF)
    for i in range(LAYERS * CUTS):
        out[i] = message


def reduce_parts(limits, parts, far):
    return pl.pallas_call(
        reduce_body,
        in_specs=[VMEM] * 3,
        out_specs=VMEM,
        out_shape=jax.ShapeDtypeStruct((LAYERS * CUTS, 2 * PIECE + EXTRA, LANES), BF),
        compiler_params=pltpu.CompilerParams(vmem_limit_bytes=16 << 20),
        cost_estimate=pl.CostEstimate(flops=200000, bytes_accessed=1300000, transcendentals=0),
    )(limits, parts, far)


def gradient_body(
    limits, gathered, one, two, three, act, cot,
    each, note, theirs,
    first, last, hidden, slopes, steep,
):
    seg = lax.axis_index("segment")
    packed = []
    for layer in range(LAYERS):
        tiles = []
        for t in range(CUTS):
            block = gathered[layer * CUTS + t].astype(F32)
            first[layer, t * PIECE : (t + 1) * PIECE] = block[:PIECE]
            last[layer, t * PIECE : (t + 1) * PIECE] = block[PIECE : 2 * PIECE]
            if t < 12:
                tiles.append(block[2 * PIECE : 2 * PIECE + 8, :RANK])
        packed.append(jnp.concatenate(tiles, axis=0))

    def gram_of(i, j):
        if j - i == 2:
            gram = jnp.concatenate([packed[i][RANK:], packed[j][RANK:]], axis=0)
        else:
            gram = packed[(i + 1 if j - i == 1 else 0)][:RANK]
        zero = jnp.zeros_like(gram)
        return jnp.concatenate(
            [jnp.concatenate([gram, zero], axis=1), jnp.concatenate([zero, gram], axis=1)], axis=0
        ).astype(BF)

    grams = {(i, j): gram_of(i, j) for j in range(LAYERS) for i in range(j)}

    for j in range(LAYERS):
        bottle = first[j]
        for i in range(j):
            bottle = bottle + dot(hidden[i], grams[i, j], 1, 0)
        value, slope = gelu_both(bottle)
        hidden[j] = value.astype(BF)
        steep[j] = slope
    for i in reversed(range(LAYERS)):
        spread = last[i]
        for j in range(i + 1, LAYERS):
            spread = spread + dot(slopes[j], grams[i, j], 1, 1)
        slopes[i] = (spread * steep[i]).astype(BF)

    slot = lax.broadcasted_iota(jnp.int32, (SLOTS, LANES), 0)
    live = slot < limits[:1]
    mine_h = jnp.where(live, hidden[seg].astype(F32), 0.0).T.astype(BF)
    mine_s = slopes[seg].astype(F32).T.astype(BF)

    lefts = []
    for k in range(1, LAYERS):
        peer = lax.rem(seg + LAYERS - k, LAYERS)
        lower = seg >= k
        left = jnp.where(lower, mine_s, mine_h)
        right = jnp.where(lower, hidden[peer], slopes[peer])
        mix = dot(left, right, 1, 0)
        mix = jnp.concatenate([mix[:RANK, :RANK], mix[RANK:, RANK:]], axis=0)
        lefts.append(
            jnp.concatenate([jnp.where(lower, mix, 0.0), jnp.where(lower, 0.0, mix)], axis=0)
        )
    left = jnp.concatenate(lefts, axis=1).astype(BF)
    peers = jnp.concatenate([one[...], two[...], three[...]], axis=0)
    extra = dot(left, peers, 1, 0)
    give = pl.multiple_of((1 - lax.axis_index("dp")) * LOCAL, 128)
    for e in range(2):
        rows = slice(e * RANK, (e + 1) * RANK)
        other = slice((2 + e) * RANK, (3 + e) * RANK)
        down_grad = extra[rows] + dot(mine_s[rows], act[e], 1, 0)
        up_grad = extra[other] + dot(mine_h[rows], cot[e], 1, 0)
        each[rows] = down_grad
        each[other] = up_grad
        square = jnp.sum(down_grad * down_grad + up_grad * up_grad)
        note[:, rows] = jnp.full((2 * CUTS, RANK), square, F32)
    theirs[...] = each[:, pl.ds(give, LOCAL)].astype(BF)


def gradients(limits, gathered, peers, act, cot):
    wide = (LAYERS, SLOTS, LANES)
    return pl.pallas_call(
        gradient_body,
        in_specs=[VMEM] * 7,
        out_specs=[VMEM] * 3,
        out_shape=[
            jax.ShapeDtypeStruct((4 * RANK, WIDTH), F32),
            jax.ShapeDtypeStruct((2 * CUTS, LANES), F32),
            jax.ShapeDtypeStruct((4 * RANK, LOCAL), BF),
        ],
        scratch_shapes=[
            pltpu.VMEM(wide, F32),
            pltpu.VMEM(wide, F32),
            pltpu.VMEM(wide, BF),
            pltpu.VMEM(wide, BF),
            pltpu.VMEM(wide, F32),
        ],
        compiler_params=pltpu.CompilerParams(vmem_limit_bytes=32 << 20),
        cost_estimate=pl.CostEstimate(
            flops=600000000, bytes_accessed=5000000, transcendentals=200000
        ),
    )(limits, gathered, peers[0], peers[1], peers[2], act, cot)


def scale_body(bounds, notes, each, swapped, out_down, out_up):
    core = lax.axis_index("dp")
    ours = each.at[:, pl.ds(pl.multiple_of(core * LOCAL, 128), LOCAL)]
    row = lax.broadcasted_iota(jnp.int32, (2 * CUTS, LANES), 0)
    is_own = lax.rem(row, 2) == core
    values = notes[...]

    def factors(picked):
        total = jnp.sum(jnp.where(picked, values, 0.0), axis=0, keepdims=True)
        return bounds[:1] / (jnp.sqrt(total) + 0.01)

    own = factors(is_own)
    other = factors(jnp.logical_not(is_own))

    def combined(start):
        total = None
        for e in range(2):
            rows = slice(start + e * RANK, start + (e + 1) * RANK)
            at = slice(e * RANK, e * RANK + 1)
            term = own[:, at] * ours[rows] + other[:, at] * swapped[rows].astype(F32)
            total = term if total is None else total + term
        return total

    out_down[0] = combined(0)
    out_up[0] = combined(2 * RANK)


def scaled(bounds, notes, each, swapped):
    return pl.pallas_call(
        scale_body,
        in_specs=[VMEM] * 4,
        out_specs=[VMEM] * 2,
        out_shape=[
            jax.ShapeDtypeStruct((1, RANK, LOCAL), F32),
            jax.ShapeDtypeStruct((1, RANK, LOCAL), F32),
        ],
        compiler_params=pltpu.CompilerParams(vmem_limit_bytes=16 << 20),
        cost_estimate=pl.CostEstimate(flops=300000, bytes_accessed=900000, transcendentals=0),
    )(bounds, notes, each, swapped)


def shards(act_input, cotangent, lengths, clip_scale, adapt_down, adapt_up):
    seg = lax.axis_index("segment")
    up = adapt_up[0]
    down_t = adapt_down[0].T
    messages = [jnp.where(seg + k < LAYERS, up, down_t) for k in range(1, LAYERS)]
    peers = [
        lax.ppermute(messages[k - 1], "segment", [(i, (i + k) % LAYERS) for i in range(LAYERS)])
        for k in range(1, LAYERS)
    ]
    partial = project(
        act_input, cotangent, messages[2], jnp.where(seg + 3 < LAYERS, down_t, up)
    )
    woven, limits, bounds = weave(
        lengths.reshape(1, 2), clip_scale.reshape(1, 1), partial, messages, peers
    )
    parts = lax.all_to_all(woven, "tensor", 0, 0, tiled=True)
    message = reduce_parts(limits, parts, peers[2])
    gathered = lax.all_to_all(message, ("segment", "tensor"), 0, 0, tiled=True)
    each, note, theirs = gradients(limits, gathered, peers, act_input, cotangent)
    swapped = lax.ppermute(theirs, "dp", [(0, 1), (1, 0)])
    notes = lax.all_to_all(note, ("tensor", "dp"), 0, 0, tiled=True)
    grad_down, grad_up = scaled(bounds, notes, each, swapped)
    return jnp.swapaxes(grad_down, 1, 2), grad_up


def solution(mesh):
    return jax.shard_map(
        shards,
        mesh=mesh,
        in_specs=(
            P("dp", None, "tensor"),
            P("dp", None, "tensor"),
            P("dp"),
            P("segment"),
            P("segment", "tensor", None),
            P("segment", None, "tensor"),
        ),
        out_specs=(P("segment", ("tensor", "dp"), None), P("segment", None, ("tensor", "dp"))),
        check_vma=False,
    )
```
